128 devices in a mesh: ctx: 8 (over y_lo, x), tp: 16 (over y_hi, z, core).
Axes of the slice: x: 4, y: 4 (y_hi: 2, y_lo: 2; y = y_hi * 2 + y_lo), z: 4, core: 2. Of those that a mesh axis runs over, the one named last changes fastest.
Arguments:
- hidden: bfloat16 [4, 2048, 6144], P(None, 'ctx', 'tp'), may hold values from -6 to 6
- w_query: bfloat16 [6144, 8192], P(None, 'tp'), may hold values from -0.078125 to 0.078125
- w_key: bfloat16 [6144, 8192], P(None, 'tp'), may hold values from -0.078125 to 0.078125
- w_value: bfloat16 [6144, 8192], P(None, 'tp'), may hold values from -0.078125 to 0.078125
- w_gate: bfloat16 [6144, 8192], P(None, 'tp'), may hold values from -0.078125 to 0.078125
- decay_rate: float32 [64], P('tp'), as said below
- norm_gain: float32 [8192], P('tp'), may hold values from 0.5 to 1.5
- doc_lengths: int32 [4, 4], replicated, may hold values from 1 to 1024, 2048 in all within a row
Outputs:
- attended: bfloat16 [4, 2048, 8192], P(None, 'ctx', 'tp')
The draws below stay inside these ranges and needn't reach their ends.
Inputs may be any that keep to these rules, and one draw needn't show every extreme that they name: Each head's state is multiplied by exp(-decay_rate) at every position; positive. `doc_lengths`: each sequence's documents fill its 2048 positions; the longest document of each sequence has exactly half of 2048 positions.
All inputs are finite; a program needn't handle non-finite values.
Results may differ from the reference program's by a relative error of at most 0.006.
Values may be sent and summed in bfloat16 or wider, within the bound.
No kernel may reach another device: no remote copies, remote signals or barrier semaphores. Data moves between devices by JAX's collectives and lax.ppermute only.
A program may use at most 128 MiB of HBM per device.

```python
import math
import jax
import jax.numpy as jnp
import numpy as np
from jax import lax

D = 6144
HEADS = 64
HDIM = 128
SEQS = 4
DOCS = 4
SEG = 256
HD = 8192
LEN = 2048
N_CTX = 8


def draw_decay_rate(key, part):
    key = jax.random.fold_in(key, 7)
    pick_key, fast_key, slow_key = jax.random.split(key, 3)
    fast_share = 0.5
    slow_low = 0.1
    slow_high = 2.0
    chosen = jax.random.uniform(pick_key, (HEADS,), jnp.float32) < fast_share
    fast_rate = jnp.exp(jax.random.uniform(fast_key, (HEADS,), jnp.float32, math.log(1.0 / 50.0), math.log(1.0 / 30.0)))
    slow_rate = jnp.exp(jax.random.uniform(slow_key, (HEADS,), jnp.float32, math.log(slow_low), math.log(slow_high))) / float(max(LEN, 64))
    return jnp.where(chosen, fast_rate, slow_rate)


def level_of(stream_key, extent, cuts, least, high):
    factor_of, own = 1.0, jax.random.fold_in(stream_key, 6)
    for dim, blocks in cuts:
        steps = jnp.exp(jax.random.uniform(jax.random.fold_in(own, dim), (blocks,), jnp.float32, least / len(cuts), high / len(cuts)))
        factor_of = factor_of * jnp.repeat(steps, extent[dim] // blocks).reshape([-1 if axis == dim else 1 for axis in range(len(extent))])
    return factor_of


def profile(count, total, reach, slope):
    portions = [(1 << 20) // math.isqrt(grade ** slope) + 1 for grade in range(2, count + 1)]
    spare, given = total - reach - (count - 1), [1] * (count - 1)
    while spare > 0:
        movable = [i for i in range(count - 1) if given[i] < reach]
        pool, budget = sum([portions[i] for i in movable]), spare
        for i in movable:
            more = min(reach - given[i], max(1, budget * portions[i] // pool), spare)
            given[i] = given[i] + more
            spare = spare - more
    return np.array([reach] + given)


def uneven(key, number_of, total, bound, lean):
    if number_of == 2:
        one = jax.random.randint(key, (), max(1, total - bound), min(bound, total - 1) + 1)
        return jnp.stack([one, total - one])
    sizes = jnp.asarray(profile(number_of, total, bound, lean), jnp.int32)
    couples = (number_of - 1) // 2
    donor, sink = sizes[1:1 + 2 * couples:2], sizes[2:2 + 2 * couples:2]
    slack = jnp.minimum(donor - 1, bound - sink)
    shifted = jax.random.randint(jax.random.fold_in(key, 1), (couples,), 0, 1 << 20) % (slack + 1)
    sizes = sizes.at[1:1 + 2 * couples:2].set(donor - shifted).at[2:2 + 2 * couples:2].set(sink + shifted)
    return sizes[jax.random.permutation(jax.random.fold_in(key, 2), number_of)]


def gaussian(key, extent, scale, limit, shards=(), dtype=jnp.bfloat16):
    factor_of = level_of(key, extent, shards, -0.22, 0.18) if shards else 1.0
    entries = jax.random.normal(key, extent, jnp.float32) * scale * factor_of
    return jnp.minimum(jnp.maximum(entries, -limit), limit).astype(dtype)


def setup_inputs(seed: int = 0) -> dict:
    key_of = jax.random.split(jax.random.key(seed), 9)
    hidden = gaussian(key_of[0], (SEQS, LEN, D), 1.0, 6.0, ((1, 8), (2, 16)))
    w_query = gaussian(key_of[1], (D, HD), D ** -0.5, 0.078125, ((1, 16),))
    w_key = gaussian(key_of[2], (D, HD), D ** -0.5, 0.078125, ((1, 16),))
    w_value = gaussian(key_of[3], (D, HD), D ** -0.5, 0.078125, ((1, 16),))
    w_gate = gaussian(key_of[4], (D, HD), D ** -0.5, 0.078125, ((1, 16),))
    decay_rate = draw_decay_rate(jax.random.fold_in(key_of[8], 71), 0)
    norm_gain = jnp.clip(1.0 + 0.1 * jax.random.normal(key_of[6], (HD,), jnp.float32), 0.5, 1.5)
    doc_lengths = jax.vmap(lambda own: uneven(own, DOCS, LEN, LEN // 2, 1))(jax.random.split(key_of[7], SEQS)).reshape((SEQS, DOCS)).astype(jnp.int32)
    return {"hidden": hidden, "w_query": w_query, "w_key": w_key, "w_value": w_value, "w_gate": w_gate, "decay_rate": decay_rate, "norm_gain": norm_gain, "doc_lengths": doc_lengths}


epsilon = 1e-06

def doc_numbers(positions, lengths):
    ends = jnp.cumsum(lengths, axis=1).astype(jnp.int32)[:, :-1]
    return lax.optimization_barrier(jnp.sum((positions[None, :, None] >= ends[:, None, :]).astype(jnp.int32), axis=2)).astype(jnp.int32)

def block_terms(query, keys, values, decay, documents, before):
    block_len = query.shape[1]
    local = lax.iota(jnp.int32, block_len)
    offsets = (local[:, None] - local[None, :]).astype(jnp.float32)
    causal = offsets >= 0.0
    pair_decay = jnp.exp(-decay[:, None, None] * jnp.maximum(offsets, 0.0))
    same_doc = documents[:, :, None] == documents[:, None, :]
    allowed = jnp.logical_and(causal[None], same_doc)
    scores = jnp.einsum('sihe,sjhe->shij', query.astype(jnp.float32), keys.astype(jnp.float32))
    mixed = jnp.where(allowed[:, None], scores * pair_decay[None], 0.0).astype(jnp.bfloat16)
    inner = jnp.einsum('shij,sjhe->sihe', mixed.astype(jnp.float32), values.astype(jnp.float32))
    position = local.astype(jnp.float32)
    final_doc = documents[:, -1]
    keep_rows = (documents == final_doc[:, None]).astype(jnp.float32)
    out_decay = jnp.exp(-decay[None, :] * (block_len - 1.0 - position)[:, None])
    weighted = (keys.astype(jnp.float32) * (keep_rows[:, :, None] * out_decay[None])[..., None]).astype(jnp.bfloat16)
    block_state = jnp.einsum('sjhe,sjhf->shef', weighted.astype(jnp.float32), values.astype(jnp.float32))
    carry_keep = (final_doc == before).astype(jnp.float32)[:, None] * jnp.exp(-decay * block_len)[None, :]
    in_decay = jnp.exp(-decay[None, :] * (position + 1.0)[:, None])
    in_rows = (documents == before[:, None]).astype(jnp.float32)
    in_scale = in_rows[:, :, None] * in_decay[None]
    return (inner, block_state, carry_keep, in_scale)

def reference(hidden, w_query, w_key, w_value, w_gate, decay_rate, norm_gain, doc_lengths):
    flat = hidden.reshape(SEQS * LEN, D)

    def project(weight):
        return jnp.dot(flat, weight, preferred_element_type=jnp.float32)

    def to_blocks(total):
        shaped = jax.nn.silu(total).astype(jnp.bfloat16).reshape(SEQS, N_CTX, SEG, HEADS, HDIM)
        return jnp.transpose(shaped, (1, 0, 2, 3, 4))
    query = to_blocks(project(w_query))
    keys = to_blocks(project(w_key))
    values = to_blocks(project(w_value))
    gate_logits = project(w_gate).reshape(SEQS, LEN, HD)
    documents = doc_numbers(lax.iota(jnp.int32, LEN), doc_lengths).reshape(SEQS, N_CTX, SEG)
    documents = jnp.transpose(documents, (1, 0, 2))
    before = jnp.transpose(doc_numbers(lax.iota(jnp.int32, N_CTX) * SEG - 1, doc_lengths), (1, 0))

    def advance(state, pieces):
        block_query, block_keys, block_values, block_docs, block_before = pieces
        inner, block_state, carry_keep, in_scale = block_terms(block_query, block_keys, block_values, decay_rate, block_docs, block_before)
        carried = jnp.einsum('sihe,shef->sihf', block_query.astype(jnp.float32), state, precision=lax.Precision.HIGHEST)
        attn = inner + carried * in_scale[..., None]
        return (carry_keep[:, :, None, None] * state + block_state, attn)
    start_state = jnp.zeros((SEQS, HEADS, HDIM, HDIM), jnp.float32)
    _, stacked = lax.scan(advance, start_state, (query, keys, values, documents, before))
    attn = jnp.transpose(stacked, (1, 0, 2, 3, 4)).reshape(SEQS, LEN, HD)
    squares = lax.optimization_barrier(jnp.sum(attn * attn, axis=2))
    scale = lax.rsqrt(squares / HD + epsilon)
    return (attn * scale[:, :, None] * norm_gain * jax.nn.sigmoid(gate_logits)).astype(jnp.bfloat16)
```

```python
import functools

import jax
import jax.numpy as jnp
from jax import lax
from jax.experimental import pallas as pl
from jax.experimental.pallas import tpu as pltpu
from jax.sharding import PartitionSpec as P

EPSILON = 1e-06
BLOCK = 256
HEAD = 128
SHARD = 384
WIDTH = 512
F32 = jnp.float32
BF16 = jnp.bfloat16
ANY = pl.BlockSpec(memory_space=pl.ANY)
SMEM = pl.BlockSpec(memory_space=pltpu.SMEM)
VMEM = pl.BlockSpec(memory_space=pltpu.VMEM)


def tp_route(step):
    route = []
    for y in range(2):
        for z in range(4):
            for c in range(2):
                y2, z2, c2 = step(y, z, c)
                route.append((y * 8 + z * 2 + c, (y2 % 2) * 8 + (z2 % 4) * 2 + c2 % 2))
    return route


RING = tp_route(lambda y, z, c: (y, z + 1 - 2 * c, c))
ACROSS = tp_route(lambda y, z, c: (y + 1, z, c))
CORE = tp_route(lambda y, z, c: (y, z, c + 1))
PAIR_A = tp_route(lambda y, z, c: (y, z ^ 1, c))
PAIR_B = tp_route(lambda y, z, c: (y, 3 - z, c))


def ring(x):
    return lax.ppermute(x, "tp", RING)


def across(x):
    return lax.ppermute(x, "tp", ACROSS)


def other_core(x):
    return lax.ppermute(x, "tp", CORE)


def ahead(x, distance):
    n = lax.axis_size("ctx")
    return lax.ppermute(x, "ctx", [(i, i + distance) for i in range(n - distance)])


def doc_ends(lengths, seq):
    first = lengths[seq, 0]
    second = first + lengths[seq, 1]
    return first, second, second + lengths[seq, 2]


def doc_of(position, ends):
    return sum((position >= end).astype(jnp.int32) for end in ends)


def decay_of(rate, steps):
    return jnp.exp(-rate * steps.astype(F32))


def matmul_kernel(mode, base, n_x, n_w, *refs):
    refs = list(refs)
    take = lambda n: [refs.pop(0) for _ in range(n)]
    ids, place, lengths, decay = take(4)
    xs, ws = take(n_x), take(n_w)
    has_acc = base
    accs = take(n_w) if has_acc else []
    if mode == "qg":
        k_in, v_in, gain = take(3)
    outs = take({"acc": n_w, "kv": 4, "qg": 3}[mode])
    xbuf, wbuf, xsem, wsem = take(4)
    n_k = 2 * n_x

    def x_copy(i):
        return pltpu.make_async_copy(
            xs[i // 2].at[i % 2], xbuf.at[:, pl.ds(i * SHARD, SHARD)], xsem.at[i]
        )

    def w_copy(n, i):
        row = pl.multiple_of(ids[i] * SHARD, SHARD)
        return pltpu.make_async_copy(
            ws[n].at[pl.ds(row, SHARD), :], wbuf.at[n, pl.ds(i * SHARD, SHARD), :], wsem.at[n, i]
        )

    for i in range(n_k):
        x_copy(i).start()
        w_copy(0, i).start()
    for n in range(1, n_w):
        for i in range(n_k):
            w_copy(n, i).start()

    def product(n):
        if n == 0:
            for i in range(n_k):
                x_copy(i).wait()
        for i in range(n_k):
            w_copy(n, i).wait()
        got = jnp.dot(xbuf[...], wbuf[n], preferred_element_type=F32)
        return got + accs[n][...] if has_acc else got

    rows = xbuf.shape[0]
    seqs = rows // BLOCK
    heads = WIDTH // HEAD
    offset = place[0]
    first_seq = place[1]

    def part(s, h):
        return pl.ds(s * BLOCK, BLOCK), pl.ds(h * HEAD, HEAD)

    if mode == "acc":
        for n in range(n_w):
            outs[n][...] = product(n)
    if mode == "kv":
        k_out, v_out, s_out, sb_out = outs
        k_out[...] = jax.nn.silu(product(0)).astype(BF16)
        v_out[...] = jax.nn.silu(product(1)).astype(BF16)
        local = lax.broadcasted_iota(jnp.int32, (BLOCK, HEAD), 0)
        for s in range(seqs):
            ends = doc_ends(lengths, first_seq + s)
            keep = doc_of(local + offset, ends) == doc_of(offset + BLOCK - 1, ends)
            for h in range(heads):
                scale = jnp.where(keep, decay_of(decay[h], BLOCK - 1 - local), 0.0)
                weighted = (k_out[part(s, h)].astype(F32) * scale).astype(BF16)
                state = lax.dot_general(
                    weighted, v_out[part(s, h)], (((0,), (0,)), ((), ())), preferred_element_type=F32
                )
                s_out[s, h] = state
                sb_out[s, h] = state.astype(BF16)
    if mode == "qg":
        q_out, inner_out, gate_out = outs
        q_out[...] = jax.nn.silu(product(0)).astype(BF16)
        gate_out[...] = gain[...] * jax.nn.sigmoid(product(1))
        row = lax.broadcasted_iota(jnp.int32, (BLOCK, BLOCK), 0)
        column = lax.broadcasted_iota(jnp.int32, (BLOCK, BLOCK), 1)
        causal = row >= column
        for h in range(heads):
            pair_decay = decay_of(decay[h], jnp.maximum(row - column, 0))
            for s in range(seqs):
                ends = doc_ends(lengths, first_seq + s)
                same = doc_of(row + offset, ends) == doc_of(column + offset, ends)
                scores = lax.dot_general(
                    q_out[part(s, h)],
                    k_in[part(s, h)],
                    (((1,), (1,)), ((), ())),
                    preferred_element_type=F32,
                )
                allowed = jnp.logical_and(causal, same)
                mixed = jnp.where(allowed, scores * pair_decay, 0.0).astype(BF16)
                inner_out[part(s, h)] = jnp.dot(
                    mixed, v_in[part(s, h)], preferred_element_type=F32
                )


def matmul(mode, scalars, ids, xs, ws, accs=(), extra=()):
    rows = xs[0].shape[1]
    n_x, n_w = len(xs), len(ws)
    seqs, heads = rows // BLOCK, WIDTH // HEAD
    wide = jax.ShapeDtypeStruct((rows, WIDTH), F32)
    half = jax.ShapeDtypeStruct((rows, WIDTH), BF16)
    state = (seqs, heads, HEAD, HEAD)
    outs = {
        "acc": [wide] * n_w,
        "kv": [half, half, jax.ShapeDtypeStruct(state, F32), jax.ShapeDtypeStruct(state, BF16)],
        "qg": [half, wide, wide],
    }[mode]
    k = 2 * n_x * SHARD
    return pl.pallas_call(
        functools.partial(matmul_kernel, mode, bool(accs), n_x, n_w),
        out_shape=outs,
        in_specs=[SMEM] * 4 + [ANY] * (n_x + n_w) + [VMEM] * (len(accs) + len(extra)),
        out_specs=[VMEM] * len(outs),
        scratch_shapes=[
            pltpu.VMEM((rows, k), BF16),
            pltpu.VMEM((n_w, k, WIDTH), BF16),
            pltpu.SemaphoreType.DMA((2 * n_x,)),
            pltpu.SemaphoreType.DMA((n_w, 2 * n_x)),
        ],
        compiler_params=pltpu.CompilerParams(vmem_limit_bytes=48 * 2**20),
        cost_estimate=pl.CostEstimate(
            flops=2 * rows * k * n_w * WIDTH,
            bytes_accessed=2 * k * (rows + n_w * WIDTH) + 4 * rows * n_w * WIDTH,
            transcendentals=0,
        ),
        name="project_" + mode,
    )(ids, *scalars, *xs, *ws, *accs, *extra)


def carried_share(place, lengths, decay, s, h, block):
    ends = doc_ends(lengths, place[1] + s)
    start = place[0] - block * BLOCK
    keep = doc_of(start + BLOCK - 1, ends) == doc_of(start - 1, ends)
    rate = jnp.full((8, HEAD), decay[h] * (-1.0 * BLOCK), F32)
    return jnp.where(keep, jnp.exp(rate), 0.0)[0:1, :]


def extend_kernel(place, lengths, decay, state, before, out):
    for s in range(state.shape[0]):
        for h in range(state.shape[1]):
            share = carried_share(place, lengths, decay, s, h, 0)
            out[s, h] = (state[s, h] + share * before[s, h].astype(F32)).astype(BF16)


def extend(scalars, state, before):
    return pl.pallas_call(
        extend_kernel,
        out_shape=jax.ShapeDtypeStruct(state.shape, BF16),
        in_specs=[SMEM] * 3 + [VMEM] * 2,
        out_specs=VMEM,
        name="extend",
    )(*scalars, state, before)


def combine_kernel(place, lengths, decay, query, inner, near, far, attn_out, squares_out):
    seqs, heads = near.shape[:2]
    offset = place[0]
    local = lax.broadcasted_iota(jnp.int32, (BLOCK, HEAD), 0)
    for s in range(seqs):
        ends = doc_ends(lengths, place[1] + s)
        inside = doc_of(local + offset, ends) == doc_of(offset - 1, ends)
        total = jnp.zeros((BLOCK, HEAD), F32)
        for h in range(heads):
            rows, columns = pl.ds(s * BLOCK, BLOCK), pl.ds(h * HEAD, HEAD)
            share = carried_share(place, lengths, decay, s, h, 1) * carried_share(
                place, lengths, decay, s, h, 2
            )
            incoming = near[s, h].astype(F32) + share * far[s, h].astype(F32)
            high = incoming.astype(BF16)
            low = (incoming - high.astype(F32)).astype(BF16)
            q = query[rows, columns]
            carried = jnp.dot(q, high, preferred_element_type=F32)
            carried = carried + jnp.dot(q, low, preferred_element_type=F32)
            scale = jnp.where(inside, decay_of(decay[h], local + 1), 0.0)
            attn = inner[rows, columns] + carried * scale
            attn_out[rows, columns] = attn
            total = total + attn * attn
        line = jnp.sum(jnp.transpose(total), axis=0, keepdims=True)
        squares_out[:, pl.ds(s * BLOCK, BLOCK)] = jnp.broadcast_to(line, (8, BLOCK))


def combine(scalars, query, inner, near, far):
    rows = query.shape[0]
    return pl.pallas_call(
        combine_kernel,
        out_shape=[
            jax.ShapeDtypeStruct((rows, WIDTH), F32),
            jax.ShapeDtypeStruct((8, rows), F32),
        ],
        in_specs=[SMEM] * 3 + [VMEM] * 4,
        out_specs=[VMEM] * 2,
        name="combine",
    )(*scalars, query, inner, near, far)


def finish_kernel(width_all, attn, gate, squares, *refs):
    out = refs[-1]
    rows = attn.shape[0]
    mean = squares[0:1, :] * (1.0 / width_all)
    scale = jnp.transpose(jnp.broadcast_to(lax.rsqrt(mean + EPSILON), (HEAD, rows)))
    for h in range(WIDTH // HEAD):
        columns = pl.ds(h * HEAD, HEAD)
        got = (attn[:, columns] * scale * gate[:, columns]).astype(BF16)
        out[:, :, columns] = got.reshape(out.shape[0], BLOCK, HEAD)


def finish(attn, gate, squares, seqs, part, so_far=None):
    rows = attn.shape[0]
    count = rows // BLOCK
    width_all = WIDTH * lax.axis_size("tp")
    more = [] if so_far is None else [so_far]
    return pl.pallas_call(
        functools.partial(finish_kernel, width_all),
        grid=(1,),
        out_shape=jax.ShapeDtypeStruct((seqs, BLOCK, WIDTH), BF16),
        in_specs=[
            pl.BlockSpec((rows, WIDTH), lambda i: (0, 0)),
            pl.BlockSpec((rows, WIDTH), lambda i: (0, 0)),
            pl.BlockSpec((8, rows), lambda i: (0, 0)),
        ]
        + [ANY] * len(more),
        out_specs=pl.BlockSpec((count, BLOCK, WIDTH), lambda i: (part, 0, 0)),
        input_output_aliases={3: 0} if more else {},
        name="finish",
    )(attn, gate, squares, *more)


def all_sum(x):
    for route in (CORE, ACROSS, PAIR_A, PAIR_B):
        x = x + lax.ppermute(x, "tp", route)
    return x


def on_device(hidden, w_query, w_key, w_value, w_gate, decay_rate, norm_gain, doc_lengths):
    seqs = hidden.shape[0]
    me = lax.axis_index("tp")
    my_y, my_z, my_c = me // 8, (me // 2) % 4, me % 2
    offset = lax.axis_index("ctx") * BLOCK
    gain = norm_gain.reshape(1, WIDTH)

    def held(flip, j, core):
        y = (my_y + flip) % 2
        c = (my_c + core) % 2
        z = (my_z + j * (2 * c - 1) + 4) % 4
        return y * 8 + z * 2 + c

    half = seqs // 2
    part_y = hidden[:half].reshape(half * BLOCK, SHARD)
    part_z = hidden[half:].reshape(half * BLOCK, SHARD)

    a = [jnp.stack([part_y, across(part_y)])]
    for _ in range(3):
        a.append(ring(a[-1]))
    b = [other_core(x) for x in a]
    r = [part_z]
    for _ in range(3):
        r.append(ring(r[-1]))
    z_near = [jnp.stack(r[:2]), jnp.stack(r[2:])]
    z_far = [across(x) for x in z_near]
    z_near_other = [other_core(x) for x in z_near]
    z_far_other = [other_core(x) for x in z_far]

    def y_ids(steps):
        return jnp.stack([held(f, j, core) for core in (0, 1) for j in steps for f in (0, 1)])

    def z_ids(flip):
        return jnp.stack([held(flip, j, core) for core in (0, 1) for j in range(4)])

    pieces = [
        (
            (a[:2] + b[:2], y_ids((0, 1))),
            (a[2:] + b[2:], y_ids((2, 3))),
        ),
        (
            (z_near + z_near_other, z_ids(0)),
            (z_far + z_far_other, z_ids(1)),
        ),
    ]
    weights = [w_key, w_value, w_query, w_gate]
    out = None
    for part, ((xs1, ids1), (xs2, ids2)) in enumerate(pieces):
        place = jnp.stack([offset, jnp.int32(part * half)])
        scalars = (place, doc_lengths, decay_rate)
        acc = matmul("acc", scalars, ids1, xs1, weights)
        keys, values, state, state_half = matmul("kv", scalars, ids2, xs2, weights[:2], acc[:2])
        before = ahead(state_half, 1)
        query, inner, gate = matmul(
            "qg", scalars, ids2, xs2, weights[2:], acc[2:], (keys, values, gain)
        )
        longer = extend(scalars, state, before)
        near, far = ahead(longer, 1), ahead(longer, 3)
        attn, squares = combine(scalars, query, inner, near, far)
        out = finish(attn, gate, all_sum(squares), seqs, part, out)
    return out


def solution(mesh):
    in_specs = (
        P(None, "ctx", "tp"),
        P(None, "tp"),
        P(None, "tp"),
        P(None, "tp"),
        P(None, "tp"),
        P("tp"),
        P("tp"),
        P(),
    )
    out_specs = P(None, "ctx", "tp")
    return jax.shard_map(
        on_device, mesh=mesh, in_specs=in_specs, out_specs=out_specs, check_vma=False
    )
```

```python
import functools

import jax
import jax.numpy as jnp
from jax import lax
from jax.experimental import pallas as pl
from jax.experimental.pallas import tpu as pltpu
from jax.sharding import PartitionSpec as P

EPSILON = 1e-06
BLOCK = 256
HEAD = 128
SHARD = 384
WIDTH = 512
LIMIT = 16
F32 = jnp.float32
BF16 = jnp.bfloat16
ANY = pl.BlockSpec(memory_space=pl.ANY)
HBM = pl.BlockSpec(memory_space=pltpu.HBM)
SMEM = pl.BlockSpec(memory_space=pltpu.SMEM)
VMEM = pl.BlockSpec(memory_space=pltpu.VMEM)
PIECES = [(0, 0), (0, 1), (1, 0), (0, 2), (1, 1), (0, 3), (1, 2), (1, 3)]
PIECE = 2 * SHARD


def tp_route(step):
    route = []
    for y in range(2):
        for z in range(4):
            for c in range(2):
                y2, z2, c2 = step(y, z, c)
                route.append((y * 8 + z * 2 + c, (y2 % 2) * 8 + (z2 % 4) * 2 + c2 % 2))
    return route


RING = tp_route(lambda y, z, c: (y, z + 1 - 2 * c, c))
ACROSS = tp_route(lambda y, z, c: (y + 1, z, c))
CORE = tp_route(lambda y, z, c: (y, z, c + 1))
PAIR_A = tp_route(lambda y, z, c: (y, z ^ 1, c))
PAIR_B = tp_route(lambda y, z, c: (y, 3 - z, c))


def ring(x):
    return lax.ppermute(x, "tp", RING)


def across(x):
    return lax.ppermute(x, "tp", ACROSS)


def other_core(x):
    return lax.ppermute(x, "tp", CORE)


def ahead(x, distance):
    n = lax.axis_size("ctx")
    return lax.ppermute(x, "ctx", [(i, i + distance) for i in range(n - distance)])


def doc_ends(lengths, seq):
    first = lengths[seq, 0]
    second = first + lengths[seq, 1]
    return first, second, second + lengths[seq, 2]


def doc_of(position, ends):
    return sum((position >= end).astype(jnp.int32) for end in ends)


def decay_of(rate, steps):
    return jnp.exp(-rate * steps.astype(F32))


def project_kernel(mode, first_seq, plan, *refs):
    n_x, parts, loads, n_held, n_w, n_acc = plan
    refs = list(refs)
    take = lambda n: [refs.pop(0) for _ in range(n)]
    meta, lengths, decay = take(3)
    xs = take(n_x)
    held = take(n_held)
    weights = take(4) if loads else []
    accs = take(n_acc)
    if mode == "qg":
        k_in, v_in, gain = take(3)
    outs = take({"first": 8, "more": n_acc, "kv": 3, "qg": 3}[mode])
    loaded = take(len(loads))
    xbuf, xsem, wsem = take(3)
    held = held + loaded

    def x_copies(p, i):
        return [
            pltpu.make_async_copy(
                xs[array] if index is None else xs[array].at[index],
                xbuf.at[p, :, pl.ds((2 * i + core) * SHARD, SHARD)],
                xsem.at[p, 2 * i + core],
            )
            for core, (array, index) in enumerate(parts[p][i][0])
        ]

    def w_copies(i, n):
        return [
            pltpu.make_async_copy(
                weights[n].at[pl.ds(pl.multiple_of(meta[1 + 2 * loads[i] + core] * SHARD, SHARD), SHARD), :],
                loaded[i].at[n, pl.ds(core * SHARD, SHARD), :],
                wsem.at[i, n, core],
            )
            for core in (0, 1)
        ]

    for p in range(len(parts)):
        for i in range(len(parts[p])):
            for copy in x_copies(p, i):
                copy.start()
    for i in range(len(loads)):
        for n in range(4):
            for copy in w_copies(i, n):
                copy.start()

    def product(p, n, acc):
        total = None if acc is None else acc[...]
        for i, (_, w) in enumerate(parts[p]):
            if n in (0, 2 if mode == "qg" else 0):
                for copy in x_copies(p, i):
                    copy.wait()
            if mode == "first":
                for copy in w_copies(0, n):
                    copy.wait()
            got = jnp.dot(
                xbuf[p, :, pl.ds(i * PIECE, PIECE)], held[w][n], preferred_element_type=F32
            )
            total = got if total is None else total + got
        return total

    offset = meta[0]

    def part(s, h):
        return pl.ds(s * BLOCK, BLOCK), pl.ds(h * HEAD, HEAD)

    heads = WIDTH // HEAD
    if mode == "first":
        half = xbuf.shape[1] // 2
        for n in range(4):
            got = product(0, n, None)
            outs[n][...] = got[:half]
            outs[4 + n][...] = got[half:]
    if mode == "more":
        for p in range(len(parts)):
            for n in range(4):
                outs[4 * p + n][...] = product(p, n, accs[4 * p + n])
    if mode == "kv":
        k_out, v_out, s_out = outs
        k_out[...] = jax.nn.silu(product(0, 0, accs[0])).astype(BF16)
        v_out[...] = jax.nn.silu(product(0, 1, accs[1])).astype(BF16)
        local = lax.broadcasted_iota(jnp.int32, (BLOCK, HEAD), 0)
        for s in range(s_out.shape[0]):
            ends = doc_ends(lengths, first_seq + s)
            keep = doc_of(local + offset, ends) == doc_of(offset + BLOCK - 1, ends)
            for h in range(heads):
                scale = jnp.where(keep, decay_of(decay[h], BLOCK - 1 - local), 0.0)
                weighted = (k_out[part(s, h)].astype(F32) * scale).astype(BF16)
                s_out[s, h] = lax.dot_general(
                    weighted, v_out[part(s, h)], (((0,), (0,)), ((), ())), preferred_element_type=F32
                )
    if mode == "qg":
        q_out, inner_out, gate_out = outs
        q_out[...] = jax.nn.silu(product(0, 2, accs[0])).astype(BF16)
        gate_out[...] = gain[...] * jax.nn.sigmoid(product(0, 3, accs[1]))
        row = lax.broadcasted_iota(jnp.int32, (BLOCK, BLOCK), 0)
        column = lax.broadcasted_iota(jnp.int32, (BLOCK, BLOCK), 1)
        causal = row >= column
        for h in range(heads):
            pair_decay = decay_of(decay[h], jnp.maximum(row - column, 0))
            for s in range(q_out.shape[0] // BLOCK):
                ends = doc_ends(lengths, first_seq + s)
                same = doc_of(row + offset, ends) == doc_of(column + offset, ends)
                scores = lax.dot_general(
                    q_out[part(s, h)],
                    k_in[part(s, h)],
                    (((1,), (1,)), ((), ())),
                    preferred_element_type=F32,
                )
                allowed = jnp.logical_and(causal, same)
                mixed = jnp.where(allowed, scores * pair_decay, 0.0).astype(BF16)
                inner_out[part(s, h)] = jnp.dot(
                    mixed, v_in[part(s, h)], preferred_element_type=F32
                )
    done = 1 if mode == "first" else 0
    for i in range(done, len(loads)):
        for n in range(4):
            for copy in w_copies(i, n):
                copy.wait()


def project(mode, scalars, parts, held, weights=(), loads=(), accs=(), extra=(), first_seq=0):
    arrays, plan_parts, used = [], [], []
    for pieces in parts:
        plan = []
        for (mine, other, index), number in pieces:
            for x in (mine, other):
                if all(x is not y for y in arrays):
                    arrays.append(x)
            where = [
                ([x is y for y in arrays].index(True), index) for x in (mine, other)
            ]
            if number in held and number not in used:
                used.append(number)
            plan.append((where, number))
        plan_parts.append(plan)
    numbers = used + list(loads)
    plan_parts = [[(where, numbers.index(number)) for where, number in plan] for plan in plan_parts]
    rows = arrays[0].shape[-2]
    half = jax.ShapeDtypeStruct((rows, WIDTH), BF16)
    wide = pltpu.VMEM((rows, WIDTH), F32)
    state = jax.ShapeDtypeStruct((rows // BLOCK, WIDTH // HEAD, HEAD, HEAD), F32)
    outs = {
        "first": [pltpu.VMEM((rows // 2, WIDTH), F32)] * 8,
        "more": [wide] * len(accs),
        "kv": [half, half, state],
        "qg": [half, wide, wide],
    }[mode]
    n_outs = len(outs)
    outs = outs + [pltpu.VMEM((4, PIECE, WIDTH), BF16)] * len(loads)
    most = max(len(p) for p in plan_parts)
    loading = [pltpu.with_memory_space_constraint(w, pltpu.HBM) for w in weights] if loads else []
    before = 3 + len(arrays) + len(used) + len(loading)
    aliases = {before + n: n for n in range(len(accs))} if mode == "more" else {}
    plan = (len(arrays), plan_parts, list(loads), len(used), 4, len(accs))
    got = pl.pallas_call(
        functools.partial(project_kernel, mode, first_seq, plan),
        out_shape=outs,
        in_specs=[SMEM] * 3
        + [ANY] * len(arrays)
        + [VMEM] * len(used)
        + [HBM] * len(loading)
        + [VMEM] * (len(accs) + len(extra)),
        out_specs=[VMEM] * len(outs),
        scratch_shapes=[
            pltpu.VMEM((len(parts), rows, most * PIECE), BF16),
            pltpu.SemaphoreType.DMA((len(parts), 2 * most)),
            pltpu.SemaphoreType.DMA((max(1, len(loads)), 4, 2)),
        ],
        input_output_aliases=aliases,
        compiler_params=pltpu.CompilerParams(vmem_limit_bytes=LIMIT * 2**20),
        cost_estimate=pl.CostEstimate(
            flops=2 * rows * PIECE * sum(len(p) for p in parts) * (4 if mode in ("first", "more") else 2) * WIDTH,
            bytes_accessed=2 * rows * PIECE,
            transcendentals=0,
        ),
        name="project_" + mode,
    )(*scalars, *arrays, *[held[n] for n in used], *loading, *accs, *extra)
    held.update(zip(loads, got[n_outs:]))
    return got[:n_outs]


def carried_share(meta, lengths, decay, s, h, block):
    ends = doc_ends(lengths, s)
    start = meta[0] - block * BLOCK
    keep = doc_of(start + BLOCK - 1, ends) == doc_of(start - 1, ends)
    rate = jnp.full((8, HEAD), decay[h] * (-1.0 * BLOCK), F32)
    return jnp.where(keep, jnp.exp(rate), 0.0)[0:1, :]


def extend_kernel(first_seq, meta, lengths, decay, state, before, out):
    for s in range(state.shape[0]):
        for h in range(state.shape[1]):
            share = carried_share(meta, lengths, decay, first_seq + s, h, 0)
            out[s, h] = (state[s, h] + share * before[s, h].astype(F32)).astype(BF16)


def extend(scalars, state, before, first_seq):
    return pl.pallas_call(
        functools.partial(extend_kernel, first_seq),
        out_shape=jax.ShapeDtypeStruct(state.shape, BF16),
        in_specs=[SMEM] * 3 + [VMEM] * 2,
        out_specs=VMEM,
        compiler_params=pltpu.CompilerParams(vmem_limit_bytes=LIMIT * 2**20),
        name="extend",
    )(*scalars, state, before)


def round_kernel(x, out):
    out[...] = x[...].astype(BF16)


def rounded(x):
    return pl.pallas_call(
        round_kernel,
        out_shape=jax.ShapeDtypeStruct(x.shape, BF16),
        in_specs=[VMEM],
        out_specs=VMEM,
        compiler_params=pltpu.CompilerParams(vmem_limit_bytes=LIMIT * 2**20),
        name="round",
    )(x)


def combine_kernel(first_seq, meta, lengths, decay, query, inner, near, far, attn_out, squares_out):
    seqs, heads = near.shape[:2]
    offset = meta[0]
    local = lax.broadcasted_iota(jnp.int32, (BLOCK, HEAD), 0)
    for s in range(seqs):
        ends = doc_ends(lengths, first_seq + s)
        inside = doc_of(local + offset, ends) == doc_of(offset - 1, ends)
        total = jnp.zeros((BLOCK, HEAD), F32)
        rows = pl.ds(s * BLOCK, BLOCK)
        for h in range(heads):
            columns = pl.ds(h * HEAD, HEAD)
            share = carried_share(meta, lengths, decay, first_seq + s, h, 1)
            share = share * carried_share(meta, lengths, decay, first_seq + s, h, 2)
            incoming = near[s, h].astype(F32) + share * far[s, h].astype(F32)
            high = incoming.astype(BF16)
            low = (incoming - high.astype(F32)).astype(BF16)
            q = query[rows, columns]
            carried = jnp.dot(q, high, preferred_element_type=F32)
            carried = carried + jnp.dot(q, low, preferred_element_type=F32)
            scale = jnp.where(inside, decay_of(decay[h], local + 1), 0.0)
            attn = inner[rows, columns] + carried * scale
            attn_out[rows, columns] = attn
            total = total + attn * attn
        line = jnp.sum(jnp.transpose(total), axis=0, keepdims=True)
        for i in range(BLOCK // HEAD):
            squares_out[pl.ds(s * (BLOCK // HEAD) + i, 1), :] = line[:, i * HEAD : (i + 1) * HEAD]


def combine(scalars, query, inner, near, far, first_seq):
    rows = query.shape[0]
    return pl.pallas_call(
        functools.partial(combine_kernel, first_seq),
        out_shape=[
            pltpu.VMEM((rows, WIDTH), F32),
            jax.ShapeDtypeStruct((rows // HEAD, HEAD), F32),
        ],
        in_specs=[SMEM] * 3 + [VMEM] * 4,
        out_specs=[VMEM] * 2,
        compiler_params=pltpu.CompilerParams(vmem_limit_bytes=LIMIT * 2**20),
        name="combine",
    )(*scalars, query, inner, near, far)


def finish_kernel(width_all, attn_y, attn_z, gate_y, gate_z, squares, out):
    attns, gates = (attn_y, attn_z), (gate_y, gate_z)
    half = out.shape[0] // 2
    per = BLOCK // HEAD
    scales = lax.rsqrt(squares[...] * (1.0 / width_all) + EPSILON)
    for i in range(scales.shape[0]):
        scale = jnp.transpose(jnp.broadcast_to(scales[i : i + 1, :], (HEAD, HEAD)))
        s, r = i // per, i % per
        rows = pl.ds((s % half) * BLOCK + r * HEAD, HEAD)
        for h in range(WIDTH // HEAD):
            columns = pl.ds(h * HEAD, HEAD)
            got = attns[s // half][rows, columns] * scale * gates[s // half][rows, columns]
            out[s, pl.ds(r * HEAD, HEAD), columns] = got.astype(BF16)


def finish(attns, gates, squares):
    width_all = WIDTH * lax.axis_size("tp")
    seqs = 2 * attns[0].shape[0] // BLOCK
    return pl.pallas_call(
        functools.partial(finish_kernel, width_all),
        out_shape=jax.ShapeDtypeStruct((seqs, BLOCK, WIDTH), BF16),
        in_specs=[VMEM] * 5,
        out_specs=VMEM,
        compiler_params=pltpu.CompilerParams(vmem_limit_bytes=LIMIT * 2**20),
        name="finish",
    )(*attns, *gates, squares)


def stack_kernel(first, second, out, sems):
    copies = [pltpu.make_async_copy(x, out.at[i], sems.at[i]) for i, x in enumerate((first, second))]
    for copy in copies:
        copy.start()
    for copy in copies:
        copy.wait()


def stack(first, second):
    return pl.pallas_call(
        stack_kernel,
        out_shape=pltpu.HBM((2, *first.shape), first.dtype),
        in_specs=[ANY] * 2,
        out_specs=HBM,
        scratch_shapes=[pltpu.SemaphoreType.DMA((2,))],
        compiler_params=pltpu.CompilerParams(vmem_limit_bytes=2**20),
        name="stack",
    )(first, second)


def add_kernel(first, second, out):
    out[...] = first[...] + second[...]


def add(first, second):
    return pl.pallas_call(
        add_kernel,
        out_shape=jax.ShapeDtypeStruct(first.shape, first.dtype),
        in_specs=[VMEM] * 2,
        out_specs=VMEM,
        compiler_params=pltpu.CompilerParams(vmem_limit_bytes=2**20),
        name="add",
    )(first, second)


def join_kernel(first, second, out):
    half = first.shape[0]
    out[pl.ds(0, half), :] = first[...]
    out[pl.ds(half, half), :] = second[...]


def join(first, second):
    return pl.pallas_call(
        join_kernel,
        out_shape=jax.ShapeDtypeStruct((2 * first.shape[0], first.shape[1]), first.dtype),
        in_specs=[VMEM] * 2,
        out_specs=VMEM,
        compiler_params=pltpu.CompilerParams(vmem_limit_bytes=2**20),
        name="join",
    )(first, second)


def all_sum(x):
    for route in (CORE, ACROSS, PAIR_A, PAIR_B):
        x = add(x, lax.ppermute(x, "tp", route))
    return x


def in_order(*groups):
    return lax.optimization_barrier(groups)


def on_device(hidden, w_query, w_key, w_value, w_gate, decay_rate, norm_gain, doc_lengths):
    seqs = hidden.shape[0]
    me = lax.axis_index("tp")
    my_y, my_z, my_c = me // 8, (me // 2) % 4, me % 2
    meta = [lax.axis_index("ctx") * BLOCK]
    gain = norm_gain.reshape(1, WIDTH)
    for flip, j in PIECES:
        for core in (0, 1):
            c = (my_c + core) % 2
            z = (my_z + j * (2 * c - 1) + 4) % 4
            meta.append((my_y + flip) % 2 * 8 + z * 2 + c)
    scalars = (jnp.stack(meta), doc_lengths, decay_rate)
    half = seqs // 2
    rows = hidden.reshape(seqs * BLOCK, SHARD)
    part_y, part_z = rows[: half * BLOCK], rows[half * BLOCK :]
    weights = [w_key, w_value, w_query, w_gate]
    held = {}

    def at(flip, j):
        return PIECES.index((flip, j))

    def one(x, flip, j):
        return [((x, other_core(x), None), at(flip, j))]

    def two(x, j):
        other = other_core(x)
        return [((x, other, flip), at(flip, j)) for flip in (0, 1)]

    y0, r1 = across(part_y), ring(part_z)
    acc = project("first", scalars, [one(rows, 0, 0)], held, weights, [0, 1, 2])
    acc, y0, r1, part_z = in_order(acc, y0, r1, part_z)

    a1, r2, far0 = ring(stack(part_y, y0)), ring(r1), across(part_z)
    acc = project("more", scalars, [one(y0, 1, 0), one(r1, 0, 1)], held, weights, [3, 4], acc)
    acc, a1, r2, far0, r1 = in_order(acc, a1, r2, far0, r1)

    a2, r3, far1 = ring(a1), ring(r2), across(r1)
    acc = project(
        "more", scalars, [two(a1, 1), one(r2, 0, 2) + one(far0, 1, 0)], held, weights, [5, 6], acc
    )
    acc, a2, r3, far1, r2 = in_order(acc, a2, r3, far1, r2)

    a3, far2 = ring(a2), across(r2)
    acc = project(
        "more", scalars, [two(a2, 2), one(r3, 0, 3) + one(far1, 1, 1)], held, weights, [7], acc
    )
    acc, a3, far2, r3 = in_order(acc, a3, far2, r3)

    far3 = across(r3)
    last_y = [two(a3, 3)]
    keys_y, values_y, state_y = project("kv", scalars, last_y, held, accs=acc[:2])
    before_y = ahead(rounded(state_y), 1)
    acc_z = project("more", scalars, [one(far2, 1, 2)], held, accs=in_order(acc[4:], state_y)[0])
    acc_z, far3 = in_order(acc_z, far3)

    last_z = [one(far3, 1, 3)]
    keys_z, values_z, state_z = project("kv", scalars, last_z, held, accs=acc_z[:2], first_seq=half)
    before_z = ahead(rounded(state_z), 1)
    acc_y, before_y, state_z = in_order(acc[2:4], before_y, state_z)
    longer_y = extend(scalars, state_y, before_y, 0)
    near_y, far_y = ahead(longer_y, 1), ahead(longer_y, 3)
    query_y, inner_y, gate_y = project(
        "qg", scalars, last_y, held, accs=acc_y, extra=(keys_y, values_y, gain)
    )
    query_y, before_z, acc_q = in_order(query_y, before_z, acc_z[2:])
    longer_z = extend(scalars, state_z, before_z, half)
    near_z, far_z = ahead(longer_z, 1), ahead(longer_z, 3)
    query_z, inner_z, gate_z = project(
        "qg", scalars, last_z, held, accs=acc_q, extra=(keys_z, values_z, gain), first_seq=half
    )
    query_z, near_y, far_y = in_order(query_z, near_y, far_y)
    attn_y, squares_y = combine(scalars, query_y, inner_y, near_y, far_y, 0)
    squares_y, near_z, far_z = in_order(squares_y, near_z, far_z)
    attn_z, squares_z = combine(scalars, query_z, inner_z, near_z, far_z, half)
    squares = all_sum(join(squares_y, squares_z))
    return finish((attn_y, attn_z), (gate_y, gate_z), squares)


def solution(mesh):
    in_specs = (
        P(None, "ctx", "tp"),
        P(None, "tp"),
        P(None, "tp"),
        P(None, "tp"),
        P(None, "tp"),
        P("tp"),
        P("tp"),
        P(),
    )
    out_specs = P(None, "ctx", "tp")
    return jax.shard_map(
        on_device, mesh=mesh, in_specs=in_specs, out_specs=out_specs, check_vma=False
    )
```

```python
import functools

import jax
import jax.numpy as jnp
from jax import lax
from jax.experimental import pallas as pl
from jax.experimental.pallas import tpu as pltpu
from jax.sharding import PartitionSpec as P

EPSILON = 1e-06
BLOCK = 256
HEAD = 128
SHARD = 384
WIDTH = 512
LIMIT = 16
F32 = jnp.float32
BF16 = jnp.bfloat16
ANY = pl.BlockSpec(memory_space=pl.ANY)
HBM = pl.BlockSpec(memory_space=pltpu.HBM)
SMEM = pl.BlockSpec(memory_space=pltpu.SMEM)
VMEM = pl.BlockSpec(memory_space=pltpu.VMEM)
PIECES = [(0, 0), (1, 0), (0, 1), (0, 2), (1, 1), (0, 3), (1, 2), (1, 3)]
PIECE = 2 * SHARD
CTX = 1 + 2 * len(PIECES)


def tp_route(step):
    route = []
    for y in range(2):
        for z in range(4):
            for c in range(2):
                y2, z2, c2 = step(y, z, c)
                route.append((y * 8 + z * 2 + c, (y2 % 2) * 8 + (z2 % 4) * 2 + c2 % 2))
    return route


RING = tp_route(lambda y, z, c: (y, z + 1 - 2 * c, c))
ACROSS = tp_route(lambda y, z, c: (y + 1, z, c))
CORE = tp_route(lambda y, z, c: (y, z, c + 1))
PAIR_A = tp_route(lambda y, z, c: (y, z ^ 1, c))
PAIR_B = tp_route(lambda y, z, c: (y, 3 - z, c))


def ring(x):
    return lax.ppermute(x, "tp", RING)


def across(x):
    return lax.ppermute(x, "tp", ACROSS)


def other_core(x):
    return lax.ppermute(x, "tp", CORE)


def ahead(x, distance):
    n = lax.axis_size("ctx")
    return lax.ppermute(x, "ctx", [(i, i + distance) for i in range(n - distance)])


def swapped(x, bit):
    return lax.ppermute(x, "ctx", [(i, i ^ bit) for i in range(lax.axis_size("ctx"))])


def doc_ends(lengths, seq):
    first = lengths[seq, 0]
    second = first + lengths[seq, 1]
    return first, second, second + lengths[seq, 2]


def doc_of(position, ends):
    return sum((position >= end).astype(jnp.int32) for end in ends)


def decay_of(rate, steps):
    return jnp.exp(-rate * steps.astype(F32))


def project_kernel(mode, first_seq, plan, *refs):
    n_x, parts, loads, n_held, n_w, n_acc = plan
    refs = list(refs)
    take = lambda n: [refs.pop(0) for _ in range(n)]
    meta, lengths, decay = take(3) if mode in ("kv", "qg") else (take(1)[0], None, None)
    xs = take(n_x)
    held = take(n_held)
    weights = take(4) if loads else []
    accs = take(n_acc)
    if mode == "qg":
        k_in, v_in, gain = take(3)
    outs = take({"first": 4, "more": len(parts) * 4, "kv": 4, "qg": 3}[mode])
    loaded = take(len(loads))
    xbuf, xsem, wsem = take(3)
    held = held + loaded

    def x_copies(p, i):
        return [
            pltpu.make_async_copy(
                xs[array] if index is None else xs[array].at[index],
                xbuf.at[p, :, pl.ds((2 * i + core) * SHARD, SHARD)],
                xsem.at[p, 2 * i + core],
            )
            for core, (array, index) in enumerate(parts[p][i][0])
        ]

    def w_copies(i, n):
        return [
            pltpu.make_async_copy(
                weights[n].at[pl.ds(pl.multiple_of(meta[1 + 2 * loads[i] + core] * SHARD, SHARD), SHARD), :],
                loaded[i].at[n, pl.ds(core * SHARD, SHARD), :],
                wsem.at[i, n, core],
            )
            for core in (0, 1)
        ]

    for p in range(len(parts)):
        for i in range(len(parts[p])):
            for copy in x_copies(p, i):
                copy.start()
    def start_loads(chosen):
        for i in chosen:
            for n in range(4):
                for copy in w_copies(i, n):
                    copy.start()

    now = len({w for pieces in parts for _, w in pieces if w >= n_held})
    waited = set()
    start_loads(range(now))

    def load(i, n):
        if i >= 0 and (i, n) not in waited:
            waited.add((i, n))
            for copy in w_copies(i, n):
                copy.wait()

    def product(p, n, acc):
        total = None if acc is None else acc[...]
        for i, (_, w) in enumerate(parts[p]):
            if n in (0, 2 if mode == "qg" else 0):
                for copy in x_copies(p, i):
                    copy.wait()
            load(w - n_held, n)
            if (p, n, i) == (0, 0, 0):
                start_loads(range(now, len(loads)))
            got = jnp.dot(
                xbuf[p, :, pl.ds(i * PIECE, PIECE)], held[w][n], preferred_element_type=F32
            )
            total = got if total is None else total + got
        return total

    offset = meta[0]

    def part(s, h):
        return pl.ds(s * BLOCK, BLOCK), pl.ds(h * HEAD, HEAD)

    heads = WIDTH // HEAD
    if mode == "first":
        for n in range(4):
            outs[n][...] = product(0, n, None)
    if mode == "more":
        for p in range(len(parts)):
            for n in range(4):
                k = 4 * p + n
                outs[k][...] = product(p, n, accs[k] if k < n_acc else None)
    if mode == "kv":
        k_out, v_out, s_out, s_half = outs
        k_out[...] = jax.nn.silu(product(0, 0, accs[0])).astype(BF16)
        v_out[...] = jax.nn.silu(product(0, 1, accs[1])).astype(BF16)
        local = lax.broadcasted_iota(jnp.int32, (BLOCK, HEAD), 0)
        for s in range(s_out.shape[0]):
            ends = doc_ends(lengths, first_seq + s)
            keep = doc_of(local + offset, ends) == doc_of(offset + BLOCK - 1, ends)
            for h in range(heads):
                scale = jnp.where(keep, decay_of(decay[h], BLOCK - 1 - local), 0.0)
                weighted = (k_out[part(s, h)].astype(F32) * scale).astype(BF16)
                state = lax.dot_general(
                    weighted, v_out[part(s, h)], (((0,), (0,)), ((), ())), preferred_element_type=F32
                )
                s_out[s, h] = state
                s_half[s, h] = state.astype(BF16)
    if mode == "qg":
        q_out, inner_out, gate_out = outs
        q_out[...] = jax.nn.silu(product(0, 2, accs[0])).astype(BF16)
        gate_out[...] = gain[...] * jax.nn.sigmoid(product(0, 3, accs[1]))
        row = lax.broadcasted_iota(jnp.int32, (BLOCK, BLOCK), 0)
        column = lax.broadcasted_iota(jnp.int32, (BLOCK, BLOCK), 1)
        causal = row >= column
        for h in range(heads):
            pair_decay = decay_of(decay[h], jnp.maximum(row - column, 0))
            for s in range(q_out.shape[0] // BLOCK):
                ends = doc_ends(lengths, first_seq + s)
                same = doc_of(row + offset, ends) == doc_of(column + offset, ends)
                scores = lax.dot_general(
                    q_out[part(s, h)],
                    k_in[part(s, h)],
                    (((1,), (1,)), ((), ())),
                    preferred_element_type=F32,
                )
                allowed = jnp.logical_and(causal, same)
                mixed = jnp.where(allowed, scores * pair_decay, 0.0).astype(BF16)
                inner_out[part(s, h)] = jnp.dot(
                    mixed, v_in[part(s, h)], preferred_element_type=F32
                )
    for i in range(len(loads)):
        for n in range(4):
            load(i, n)


def project(mode, scalars, parts, held, weights=(), loads=(), accs=(), extra=(), first_seq=0):
    arrays, plan_parts, used = [], [], []
    for pieces in parts:
        plan = []
        for (mine, other, index), number in pieces:
            for x in (mine, other):
                if all(x is not y for y in arrays):
                    arrays.append(x)
            where = [
                ([x is y for y in arrays].index(True), index) for x in (mine, other)
            ]
            if number in held and number not in used:
                used.append(number)
            plan.append((where, number))
        plan_parts.append(plan)
    numbers = used + list(loads)
    plan_parts = [[(where, numbers.index(number)) for where, number in plan] for plan in plan_parts]
    index = parts[0][0][0][2]
    rows = index.size if isinstance(index, pl.Slice) else arrays[0].shape[-2]
    half = jax.ShapeDtypeStruct((rows, WIDTH), BF16)
    wide = pltpu.VMEM((rows, WIDTH), F32)
    state = [
        jax.ShapeDtypeStruct((rows // BLOCK, WIDTH // HEAD, HEAD, HEAD), t) for t in (F32, BF16)
    ]
    outs = {
        "first": [wide] * 4,
        "more": [wide] * (4 * len(parts)),
        "kv": [half, half, *state],
        "qg": [half, wide, wide],
    }[mode]
    n_outs = len(outs)
    if mode in ("first", "more"):
        scalars = scalars[:1]
    outs = outs + [pltpu.VMEM((4, PIECE, WIDTH), BF16)] * len(loads)
    most = max(len(p) for p in plan_parts)
    if mode == "first":
        arrays = [pltpu.with_memory_space_constraint(x, pltpu.HBM) for x in arrays]
    loading = [pltpu.with_memory_space_constraint(w, pltpu.HBM) for w in weights] if loads else []
    before = len(scalars) + len(arrays) + len(used) + len(loading)
    aliases = {before + n: n for n in range(len(accs))} if mode == "more" else {}
    plan = (len(arrays), plan_parts, list(loads), len(used), 4, len(accs))
    got = pl.pallas_call(
        functools.partial(project_kernel, mode, first_seq, plan),
        out_shape=outs,
        in_specs=[SMEM] * len(scalars)
        + [HBM if mode == "first" else ANY] * len(arrays)
        + [VMEM] * len(used)
        + [HBM] * len(loading)
        + [VMEM] * (len(accs) + len(extra)),
        out_specs=[VMEM] * len(outs),
        scratch_shapes=[
            pltpu.VMEM((len(parts), rows, most * PIECE), BF16),
            pltpu.SemaphoreType.DMA((len(parts), 2 * most)),
            pltpu.SemaphoreType.DMA((max(1, len(loads)), 4, 2)),
        ],
        input_output_aliases=aliases,
        compiler_params=pltpu.CompilerParams(vmem_limit_bytes=LIMIT * 2**20),
        cost_estimate=pl.CostEstimate(
            flops=2 * rows * PIECE * sum(len(p) for p in parts) * (4 if mode in ("first", "more") else 2) * WIDTH,
            bytes_accessed=2 * rows * PIECE,
            transcendentals=0,
        ),
        name="project_" + mode,
    )(*scalars, *arrays, *[held[n] for n in used], *loading, *accs, *extra)
    held.update(zip(loads, got[n_outs:]))
    return got[:n_outs]


def carried_share(meta, lengths, decay, s, h, block):
    ends = doc_ends(lengths, s)
    start = meta[0] - block * BLOCK
    keep = doc_of(start + BLOCK - 1, ends) == doc_of(start - 1, ends)
    rate = jnp.full((8, HEAD), decay[h] * (-1.0 * BLOCK), F32)
    return jnp.where(keep, jnp.exp(rate), 0.0)[0:1, :]


def one_or(condition, share):
    return jnp.where(condition, 1.0, share)


def pair_kernel(first_seq, meta, lengths, decay, state, before, out):
    odd = meta[CTX] % 2 == 1
    for s in range(state.shape[0]):
        for h in range(state.shape[1]):
            share = functools.partial(carried_share, meta, lengths, decay, first_seq + s, h)
            mine, other = one_or(odd, share(-1)), one_or(jnp.logical_not(odd), share(0))
            out[s, h] = (mine * state[s, h] + other * before[s, h].astype(F32)).astype(BF16)


def quad_kernel(first_seq, meta, lengths, decay, state, before, out):
    odd, high = meta[CTX] % 2, meta[CTX] // 2 % 2 == 1
    for s in range(state.shape[0]):
        for h in range(state.shape[1]):
            share = functools.partial(carried_share, meta, lengths, decay, first_seq + s, h)
            mine = one_or(high, share(odd - 2) * share(odd - 3))
            other = one_or(jnp.logical_not(high), share(odd) * share(odd - 1))
            got = mine * state[s, h].astype(F32) + other * before[s, h].astype(F32)
            out[s, h] = got.astype(BF16)


def extend_kernel(first_seq, meta, lengths, decay, state, before, out):
    for s in range(state.shape[0]):
        for h in range(state.shape[1]):
            share = carried_share(meta, lengths, decay, first_seq + s, h, 0)
            out[s, h] = (state[s, h] + share * before[s, h].astype(F32)).astype(BF16)


def extend(kernel, scalars, state, before, first_seq):
    return pl.pallas_call(
        functools.partial(kernel, first_seq),
        out_shape=jax.ShapeDtypeStruct(state.shape, BF16),
        in_specs=[SMEM] * 3 + [VMEM] * 2,
        out_specs=VMEM,
        compiler_params=pltpu.CompilerParams(vmem_limit_bytes=LIMIT * 2**20),
        name="extend",
    )(*scalars, state, before)


def shares(scan, meta, share):
    if not scan:
        return [1.0, share(1) * share(2)]
    place = meta[CTX] % 4
    odd, high = place % 2 == 1, place >= 2
    first = jnp.where(odd, 1.0, jnp.zeros((1, HEAD), F32))
    second = jnp.where(high, one_or(jnp.logical_not(odd), share(1)), 0.0)
    third = one_or(place < 1, share(1)) * one_or(place < 2, share(2)) * one_or(place < 3, share(3))
    return [first, second, third]


def combine_kernel(scan, first_seq, meta, lengths, decay, query, inner, *refs):
    arrived, (attn_out, squares_out) = refs[:-2], refs[-2:]
    seqs, heads = arrived[0].shape[:2]
    offset = meta[0]
    local = lax.broadcasted_iota(jnp.int32, (BLOCK, HEAD), 0)
    for s in range(seqs):
        ends = doc_ends(lengths, first_seq + s)
        inside = doc_of(local + offset, ends) == doc_of(offset - 1, ends)
        total = jnp.zeros((BLOCK, HEAD), F32)
        rows = pl.ds(s * BLOCK, BLOCK)
        for h in range(heads):
            columns = pl.ds(h * HEAD, HEAD)
            share = functools.partial(carried_share, meta, lengths, decay, first_seq + s, h)
            incoming = sum(
                weight * x[s, h].astype(F32) for weight, x in zip(shares(scan, meta, share), arrived)
            )
            high = incoming.astype(BF16)
            low = (incoming - high.astype(F32)).astype(BF16)
            q = query[rows, columns]
            carried = jnp.dot(q, high, preferred_element_type=F32)
            carried = carried + jnp.dot(q, low, preferred_element_type=F32)
            scale = jnp.where(inside, decay_of(decay[h], local + 1), 0.0)
            attn = inner[rows, columns] + carried * scale
            attn_out[rows, columns] = attn
            total = total + attn * attn
        line = jnp.sum(jnp.transpose(total), axis=0, keepdims=True)
        for i in range(BLOCK // HEAD):
            squares_out[pl.ds(s * (BLOCK // HEAD) + i, 1), :] = line[:, i * HEAD : (i + 1) * HEAD]


def combine(scan, scalars, query, inner, arrived, first_seq):
    rows = query.shape[0]
    return pl.pallas_call(
        functools.partial(combine_kernel, scan, first_seq),
        out_shape=[
            pltpu.VMEM((rows, WIDTH), F32),
            jax.ShapeDtypeStruct((rows // HEAD, HEAD), F32),
        ],
        in_specs=[SMEM] * 3 + [VMEM] * (2 + len(arrived)),
        out_specs=[VMEM] * 2,
        compiler_params=pltpu.CompilerParams(vmem_limit_bytes=LIMIT * 2**20),
        name="combine",
    )(*scalars, query, inner, *arrived)


def finish_kernel(width_all, attn_y, attn_z, gate_y, gate_z, squares, out):
    attns, gates = (attn_y, attn_z), (gate_y, gate_z)
    half = out.shape[0] // 2
    per = BLOCK // HEAD
    scales = lax.rsqrt(squares[...] * (1.0 / width_all) + EPSILON)
    for i in range(scales.shape[0]):
        scale = jnp.transpose(jnp.broadcast_to(scales[i : i + 1, :], (HEAD, HEAD)))
        s, r = i // per, i % per
        rows = pl.ds((s % half) * BLOCK + r * HEAD, HEAD)
        for h in range(WIDTH // HEAD):
            columns = pl.ds(h * HEAD, HEAD)
            got = attns[s // half][rows, columns] * scale * gates[s // half][rows, columns]
            out[s, pl.ds(r * HEAD, HEAD), columns] = got.astype(BF16)


def finish(attns, gates, squares):
    width_all = WIDTH * lax.axis_size("tp")
    seqs = 2 * attns[0].shape[0] // BLOCK
    return pl.pallas_call(
        functools.partial(finish_kernel, width_all),
        out_shape=jax.ShapeDtypeStruct((seqs, BLOCK, WIDTH), BF16),
        in_specs=[VMEM] * 5,
        out_specs=VMEM,
        compiler_params=pltpu.CompilerParams(vmem_limit_bytes=LIMIT * 2**20),
        name="finish",
    )(*attns, *gates, squares)


def stack_kernel(first, second, out, sems):
    copies = [pltpu.make_async_copy(x, out.at[i], sems.at[i]) for i, x in enumerate((first, second))]
    for copy in copies:
        copy.start()
    for copy in copies:
        copy.wait()


def stack(first, second):
    return pl.pallas_call(
        stack_kernel,
        out_shape=pltpu.HBM((2, *first.shape), first.dtype),
        in_specs=[ANY] * 2,
        out_specs=HBM,
        scratch_shapes=[pltpu.SemaphoreType.DMA((2,))],
        compiler_params=pltpu.CompilerParams(vmem_limit_bytes=2**20),
        name="stack",
    )(first, second)


def add_kernel(first, second, out):
    out[...] = first[...] + second[...]


def add(first, second):
    return pl.pallas_call(
        add_kernel,
        out_shape=jax.ShapeDtypeStruct(first.shape, first.dtype),
        in_specs=[VMEM] * 2,
        out_specs=VMEM,
        compiler_params=pltpu.CompilerParams(vmem_limit_bytes=2**20),
        name="add",
    )(first, second)


def join_kernel(first, second, out):
    half = first.shape[0]
    out[pl.ds(0, half), :] = first[...]
    out[pl.ds(half, half), :] = second[...]


def join(first, second):
    return pl.pallas_call(
        join_kernel,
        out_shape=jax.ShapeDtypeStruct((2 * first.shape[0], first.shape[1]), first.dtype),
        in_specs=[VMEM] * 2,
        out_specs=VMEM,
        compiler_params=pltpu.CompilerParams(vmem_limit_bytes=2**20),
        name="join",
    )(first, second)


def all_sum(x):
    for route in (CORE, ACROSS, PAIR_A, PAIR_B):
        x = add(x, lax.ppermute(x, "tp", route))
    return x


def in_order(*groups):
    return lax.optimization_barrier(groups)


def on_device(hidden, w_query, w_key, w_value, w_gate, decay_rate, norm_gain, doc_lengths):
    seqs = hidden.shape[0]
    me = lax.axis_index("tp")
    my_y, my_z, my_c = me // 8, (me // 2) % 4, me % 2
    meta = [lax.axis_index("ctx") * BLOCK]
    gain = norm_gain.reshape(1, WIDTH)
    for flip, j in PIECES:
        for core in (0, 1):
            c = (my_c + core) % 2
            z = (my_z + j * (2 * c - 1) + 4) % 4
            meta.append((my_y + flip) % 2 * 8 + z * 2 + c)
    meta.append(lax.axis_index("ctx"))
    scalars = (jnp.stack(meta), doc_lengths, decay_rate)
    half = seqs // 2
    rows = hidden.reshape(seqs * BLOCK, SHARD)
    part_y, part_z = rows[: half * BLOCK], rows[half * BLOCK :]
    weights = [w_key, w_value, w_query, w_gate]
    held = {}

    def at(flip, j):
        return PIECES.index((flip, j))

    def one(x, flip, j):
        return [((x, other_core(x), None), at(flip, j))]

    def two(x, j):
        other = other_core(x)
        return [((x, other, flip), at(flip, j)) for flip in (0, 1)]

    y0, r1 = across(part_y), ring(part_z)
    rows_other = other_core(rows)
    own_y, own_z = [
        ((rows, rows_other, pl.ds(p * half * BLOCK, half * BLOCK)), at(0, 0)) for p in (0, 1)
    ]
    acc = project("first", scalars, [[own_y]], held, weights, [0, 1])
    acc, y0, r1, part_z = in_order(acc, y0, r1, part_z)

    a1, r2, far_a = ring(stack(part_y, y0)), ring(r1), across(stack(part_z, r1))
    parts = [one(y0, 1, 0), [own_z] + one(r1, 0, 1)]
    acc = project("more", scalars, parts, held, weights, [2, 3, 4], acc)
    acc, a1, r2, far_a = in_order(acc, a1, r2, far_a)

    a2, r3, far2 = ring(a1), ring(r2), across(r2)
    parts = [two(a1, 1), one(r2, 0, 2) + [(x, at(1, i)) for i, (x, _) in enumerate(two(far_a, 0))]]
    acc = project("more", scalars, parts, held, weights, [5, 6], acc)
    acc, a2, r3, far2 = in_order(acc, a2, r3, far2)

    a3, far3 = ring(a2), across(r3)
    parts = [two(a2, 2), one(r3, 0, 3) + one(far2, 1, 2)]
    acc = project("more", scalars, parts, held, weights, [7], acc)
    acc, a3, far3 = in_order(acc, a3, far3)

    last_y, last_z = [two(a3, 3)], [one(far3, 1, 3)]
    keys_y, values_y, state_y, sent_y = project("kv", scalars, last_y, held, accs=acc[:2])
    one_y = swapped(sent_y, 1)
    acc, state_y = in_order(acc, state_y)
    keys_z, values_z, state_z, sent_z = project(
        "kv", scalars, last_z, held, accs=acc[4:6], first_seq=half
    )
    before_z = ahead(sent_z, 1)
    acc, state_z = in_order(acc, state_z)
    query_y, inner_y, gate_y = project(
        "qg", scalars, last_y, held, accs=acc[2:4], extra=(keys_y, values_y, gain)
    )
    query_y, one_y, acc = in_order(query_y, one_y, acc)
    pair_y = extend(pair_kernel, scalars, state_y, one_y, 0)
    two_y = swapped(pair_y, 2)
    before_z, pair_y = in_order(before_z, pair_y)
    longer_z = extend(extend_kernel, scalars, state_z, before_z, half)
    near_z, far_z = ahead(longer_z, 1), ahead(longer_z, 3)
    acc, longer_z = in_order(acc, longer_z)
    query_z, inner_z, gate_z = project(
        "qg", scalars, last_z, held, accs=acc[6:], extra=(keys_z, values_z, gain), first_seq=half
    )
    query_z, two_y = in_order(query_z, two_y)
    four_y = ahead(extend(quad_kernel, scalars, pair_y, two_y, 0), 4)
    query_z, near_z, far_z = in_order(query_z, near_z, far_z)
    attn_z, squares_z = combine(False, scalars, query_z, inner_z, (near_z, far_z), half)
    squares_z, four_y = in_order(squares_z, four_y)
    attn_y, squares_y = combine(True, scalars, query_y, inner_y, (one_y, two_y, four_y), 0)
    squares = all_sum(join(squares_y, squares_z))
    return finish((attn_y, attn_z), (gate_y, gate_z), squares)


def solution(mesh):
    in_specs = (
        P(None, "ctx", "tp"),
        P(None, "tp"),
        P(None, "tp"),
        P(None, "tp"),
        P(None, "tp"),
        P("tp"),
        P("tp"),
        P(),
    )
    out_specs = P(None, "ctx", "tp")
    return jax.shard_map(
        on_device, mesh=mesh, in_specs=in_specs, out_specs=out_specs, check_vma=False
    )
```

```python
import functools

import jax
import jax.numpy as jnp
from jax import lax
from jax.experimental import pallas as pl
from jax.experimental.pallas import tpu as pltpu
from jax.sharding import PartitionSpec as P

EPSILON = 1e-06
BLOCK = 256
HEAD = 128
SHARD = 384
WIDTH = 512
LIMIT = 16
F32 = jnp.float32
BF16 = jnp.bfloat16
ANY = pl.BlockSpec(memory_space=pl.ANY)
HBM = pl.BlockSpec(memory_space=pltpu.HBM)
SMEM = pl.BlockSpec(memory_space=pltpu.SMEM)
VMEM = pl.BlockSpec(memory_space=pltpu.VMEM)
PIECES = [(0, 0), (1, 0), (0, 1), (0, 2), (1, 1), (0, 3), (1, 2), (1, 3)]
PIECE = 2 * SHARD
CTX = 1 + 2 * len(PIECES)


def tp_route(step):
    route = []
    for y in range(2):
        for z in range(4):
            for c in range(2):
                y2, z2, c2 = step(y, z, c)
                route.append((y * 8 + z * 2 + c, (y2 % 2) * 8 + (z2 % 4) * 2 + c2 % 2))
    return route


RING = tp_route(lambda y, z, c: (y, z + 1 - 2 * c, c))
ACROSS = tp_route(lambda y, z, c: (y + 1, z, c))
CORE = tp_route(lambda y, z, c: (y, z, c + 1))
PAIR_A = tp_route(lambda y, z, c: (y, z ^ 1, c))
PAIR_B = tp_route(lambda y, z, c: (y, 3 - z, c))


def ring(x):
    return lax.ppermute(x, "tp", RING)


def across(x):
    return lax.ppermute(x, "tp", ACROSS)


def other_core(x):
    return lax.ppermute(x, "tp", CORE)


def ahead(x, distance):
    n = lax.axis_size("ctx")
    return lax.ppermute(x, "ctx", [(i, i + distance) for i in range(n - distance)])


def swapped(x, bit):
    return lax.ppermute(x, "ctx", [(i, i ^ bit) for i in range(lax.axis_size("ctx"))])


def round_x(x, distance):
    n = lax.axis_size("ctx")
    return lax.ppermute(x, "ctx", [(i, i // 4 * 4 + (i + distance) % 4) for i in range(n)])


def doc_ends(lengths, seq):
    first = lengths[seq, 0]
    second = first + lengths[seq, 1]
    return first, second, second + lengths[seq, 2]


def doc_of(position, ends):
    return sum((position >= end).astype(jnp.int32) for end in ends)


def decay_of(rate, steps):
    return jnp.exp(-rate * steps.astype(F32))


def project_kernel(mode, first_seq, plan, *refs):
    n_x, parts, loads, n_held, n_w, n_acc = plan
    refs = list(refs)
    take = lambda n: [refs.pop(0) for _ in range(n)]
    meta, lengths, decay = take(3) if mode in ("kv", "qg") else (take(1)[0], None, None)
    xs = take(n_x)
    held = take(n_held)
    weights = take(4) if loads else []
    accs = take(n_acc)
    if mode == "qg":
        k_in, v_in, gain = take(3)
    outs = take({"first": 4, "more": len(parts) * 4, "kv": 4, "qg": 3}[mode])
    loaded = take(len(loads))
    xbuf, xsem, wsem = take(3)
    held = held + loaded

    def x_copies(p, i):
        return [
            pltpu.make_async_copy(
                xs[array] if index is None else xs[array].at[index],
                xbuf.at[p, :, pl.ds((2 * i + core) * SHARD, SHARD)],
                xsem.at[p, 2 * i + core],
            )
            for core, (array, index) in enumerate(parts[p][i][0])
        ]

    def w_copies(i, n):
        return [
            pltpu.make_async_copy(
                weights[n].at[pl.ds(pl.multiple_of(meta[1 + 2 * loads[i] + core] * SHARD, SHARD), SHARD), :],
                loaded[i].at[n, pl.ds(core * SHARD, SHARD), :],
                wsem.at[i, n, core],
            )
            for core in (0, 1)
        ]

    for p in range(len(parts)):
        for i in range(len(parts[p])):
            for copy in x_copies(p, i):
                copy.start()
    def start_loads(chosen):
        for i in chosen:
            for n in range(4):
                for copy in w_copies(i, n):
                    copy.start()

    now = len({w for pieces in parts for _, w in pieces if w >= n_held})
    waited = set()
    start_loads(range(now))

    def load(i, n):
        if i >= 0 and (i, n) not in waited:
            waited.add((i, n))
            for copy in w_copies(i, n):
                copy.wait()

    def product(p, n, acc):
        total = None if acc is None else acc[...]
        for i, (_, w) in enumerate(parts[p]):
            if n in (0, 2 if mode == "qg" else 0):
                for copy in x_copies(p, i):
                    copy.wait()
            load(w - n_held, n)
            if (p, n, i) == (0, 0, 0):
                start_loads(range(now, len(loads)))
            got = jnp.dot(
                xbuf[p, :, pl.ds(i * PIECE, PIECE)], held[w][n], preferred_element_type=F32
            )
            total = got if total is None else total + got
        return total

    offset = meta[0]

    def part(s, h):
        return pl.ds(s * BLOCK, BLOCK), pl.ds(h * HEAD, HEAD)

    heads = WIDTH // HEAD
    if mode == "first":
        for n in range(4):
            outs[n][...] = product(0, n, None)
    if mode == "more":
        for p in range(len(parts)):
            for n in range(4):
                k = 4 * p + n
                outs[k][...] = product(p, n, accs[k] if k < n_acc else None)
    if mode == "kv":
        k_out, v_out, s_out, s_half = outs
        k_out[...] = jax.nn.silu(product(0, 0, accs[0])).astype(BF16)
        v_out[...] = jax.nn.silu(product(0, 1, accs[1])).astype(BF16)
        local = lax.broadcasted_iota(jnp.int32, (BLOCK, HEAD), 0)
        for s in range(s_out.shape[0]):
            ends = doc_ends(lengths, first_seq + s)
            keep = doc_of(local + offset, ends) == doc_of(offset + BLOCK - 1, ends)
            for h in range(heads):
                scale = jnp.where(keep, decay_of(decay[h], BLOCK - 1 - local), 0.0)
                weighted = (k_out[part(s, h)].astype(F32) * scale).astype(BF16)
                state = lax.dot_general(
                    weighted, v_out[part(s, h)], (((0,), (0,)), ((), ())), preferred_element_type=F32
                )
                s_out[s, h] = state
                s_half[s, h] = state.astype(BF16)
    if mode == "qg":
        q_out, inner_out, gate_out = outs
        q_out[...] = jax.nn.silu(product(0, 2, accs[0])).astype(BF16)
        gate_out[...] = gain[...] * jax.nn.sigmoid(product(0, 3, accs[1]))
        row = lax.broadcasted_iota(jnp.int32, (BLOCK, BLOCK), 0)
        column = lax.broadcasted_iota(jnp.int32, (BLOCK, BLOCK), 1)
        causal = row >= column
        for h in range(heads):
            pair_decay = decay_of(decay[h], jnp.maximum(row - column, 0))
            for s in range(q_out.shape[0] // BLOCK):
                ends = doc_ends(lengths, first_seq + s)
                same = doc_of(row + offset, ends) == doc_of(column + offset, ends)
                scores = lax.dot_general(
                    q_out[part(s, h)],
                    k_in[part(s, h)],
                    (((1,), (1,)), ((), ())),
                    preferred_element_type=F32,
                )
                allowed = jnp.logical_and(causal, same)
                mixed = jnp.where(allowed, scores * pair_decay, 0.0).astype(BF16)
                inner_out[part(s, h)] = jnp.dot(
                    mixed, v_in[part(s, h)], preferred_element_type=F32
                )
    for i in range(len(loads)):
        for n in range(4):
            load(i, n)


def project(mode, scalars, parts, held, weights=(), loads=(), accs=(), extra=(), first_seq=0):
    arrays, plan_parts, used = [], [], []
    for pieces in parts:
        plan = []
        for (mine, other, index), number in pieces:
            for x in (mine, other):
                if all(x is not y for y in arrays):
                    arrays.append(x)
            where = [
                ([x is y for y in arrays].index(True), index) for x in (mine, other)
            ]
            if number in held and number not in used:
                used.append(number)
            plan.append((where, number))
        plan_parts.append(plan)
    numbers = used + list(loads)
    plan_parts = [[(where, numbers.index(number)) for where, number in plan] for plan in plan_parts]
    index = parts[0][0][0][2]
    rows = index.size if isinstance(index, pl.Slice) else arrays[0].shape[-2]
    half = jax.ShapeDtypeStruct((rows, WIDTH), BF16)
    wide = pltpu.VMEM((rows, WIDTH), F32)
    state = [
        jax.ShapeDtypeStruct((rows // BLOCK, WIDTH // HEAD, HEAD, HEAD), t) for t in (F32, BF16)
    ]
    outs = {
        "first": [wide] * 4,
        "more": [wide] * (4 * len(parts)),
        "kv": [half, half, *state],
        "qg": [half, wide, wide],
    }[mode]
    n_outs = len(outs)
    if mode in ("first", "more"):
        scalars = scalars[:1]
    outs = outs + [pltpu.VMEM((4, PIECE, WIDTH), BF16)] * len(loads)
    most = max(len(p) for p in plan_parts)
    if mode == "first":
        arrays = [pltpu.with_memory_space_constraint(x, pltpu.HBM) for x in arrays]
    loading = [pltpu.with_memory_space_constraint(w, pltpu.HBM) for w in weights] if loads else []
    before = len(scalars) + len(arrays) + len(used) + len(loading)
    aliases = {before + n: n for n in range(len(accs))} if mode == "more" else {}
    plan = (len(arrays), plan_parts, list(loads), len(used), 4, len(accs))
    got = pl.pallas_call(
        functools.partial(project_kernel, mode, first_seq, plan),
        out_shape=outs,
        in_specs=[SMEM] * len(scalars)
        + [HBM if mode == "first" else ANY] * len(arrays)
        + [VMEM] * len(used)
        + [HBM] * len(loading)
        + [VMEM] * (len(accs) + len(extra)),
        out_specs=[VMEM] * len(outs),
        scratch_shapes=[
            pltpu.VMEM((len(parts), rows, most * PIECE), BF16),
            pltpu.SemaphoreType.DMA((len(parts), 2 * most)),
            pltpu.SemaphoreType.DMA((max(1, len(loads)), 4, 2)),
        ],
        input_output_aliases=aliases,
        compiler_params=pltpu.CompilerParams(vmem_limit_bytes=LIMIT * 2**20),
        cost_estimate=pl.CostEstimate(
            flops=2 * rows * PIECE * sum(len(p) for p in parts) * (4 if mode in ("first", "more") else 2) * WIDTH,
            bytes_accessed=2 * rows * PIECE,
            transcendentals=0,
        ),
        name="project_" + mode,
    )(*scalars, *arrays, *[held[n] for n in used], *loading, *accs, *extra)
    held.update(zip(loads, got[n_outs:]))
    return got[:n_outs]


def carried_share(meta, lengths, decay, s, h, block):
    ends = doc_ends(lengths, s)
    start = meta[0] - block * BLOCK
    keep = doc_of(start + BLOCK - 1, ends) == doc_of(start - 1, ends)
    rate = jnp.full((8, HEAD), decay[h] * (-1.0 * BLOCK), F32)
    return jnp.where(keep, jnp.exp(rate), 0.0)[0:1, :]


def one_or(condition, share):
    return jnp.where(condition, 1.0, share)


def pair_kernel(first_seq, meta, lengths, decay, state, before, out):
    odd = meta[CTX] % 2 == 1
    for s in range(state.shape[0]):
        for h in range(state.shape[1]):
            share = functools.partial(carried_share, meta, lengths, decay, first_seq + s, h)
            mine, other = one_or(odd, share(-1)), one_or(jnp.logical_not(odd), share(0))
            out[s, h] = (mine * state[s, h] + other * before[s, h].astype(F32)).astype(BF16)


def quad_kernel(first_seq, meta, lengths, decay, state, before, out):
    odd, high = meta[CTX] % 2, meta[CTX] // 2 % 2 == 1
    for s in range(state.shape[0]):
        for h in range(state.shape[1]):
            share = functools.partial(carried_share, meta, lengths, decay, first_seq + s, h)
            mine = one_or(high, share(odd - 2) * share(odd - 3))
            other = one_or(jnp.logical_not(high), share(odd) * share(odd - 1))
            got = mine * state[s, h].astype(F32) + other * before[s, h].astype(F32)
            out[s, h] = got.astype(BF16)


def choose_kernel(meta, state, earlier, *outs):
    for distance, out in enumerate(outs, 1):
        wraps = meta[CTX] % 4 + distance >= 4
        for s in range(state.shape[0]):
            for h in range(state.shape[1]):
                out[s, h] = jnp.where(wraps, earlier[s, h], state[s, h])


def choose(scalars, state, earlier):
    return pl.pallas_call(
        choose_kernel,
        out_shape=[jax.ShapeDtypeStruct(state.shape, BF16)] * 3,
        in_specs=[SMEM] + [VMEM] * 2,
        out_specs=[VMEM] * 3,
        compiler_params=pltpu.CompilerParams(vmem_limit_bytes=LIMIT * 2**20),
        name="choose",
    )(scalars[0], state, earlier)


def extend(kernel, scalars, state, before, first_seq):
    return pl.pallas_call(
        functools.partial(kernel, first_seq),
        out_shape=jax.ShapeDtypeStruct(state.shape, BF16),
        in_specs=[SMEM] * 3 + [VMEM] * 2,
        out_specs=VMEM,
        compiler_params=pltpu.CompilerParams(vmem_limit_bytes=LIMIT * 2**20),
        name="extend",
    )(*scalars, state, before)


def shares(scan, meta, share):
    if not scan:
        return [1.0, share(1), share(1) * share(2), share(1) * share(2) * share(3)]
    place = meta[CTX] % 4
    odd, high = place % 2 == 1, place >= 2
    first = jnp.where(odd, 1.0, jnp.zeros((1, HEAD), F32))
    second = jnp.where(high, one_or(jnp.logical_not(odd), share(1)), 0.0)
    third = one_or(place < 1, share(1)) * one_or(place < 2, share(2)) * one_or(place < 3, share(3))
    return [first, second, third]


def combine_kernel(scan, first_seq, meta, lengths, decay, query, inner, *refs):
    arrived, (attn_out, squares_out) = refs[:-2], refs[-2:]
    seqs, heads = arrived[0].shape[:2]
    offset = meta[0]
    local = lax.broadcasted_iota(jnp.int32, (BLOCK, HEAD), 0)
    for s in range(seqs):
        ends = doc_ends(lengths, first_seq + s)
        inside = doc_of(local + offset, ends) == doc_of(offset - 1, ends)
        total = jnp.zeros((BLOCK, HEAD), F32)
        rows = pl.ds(s * BLOCK, BLOCK)
        for h in range(heads):
            columns = pl.ds(h * HEAD, HEAD)
            share = functools.partial(carried_share, meta, lengths, decay, first_seq + s, h)
            incoming = sum(
                weight * x[s, h].astype(F32) for weight, x in zip(shares(scan, meta, share), arrived)
            )
            high = incoming.astype(BF16)
            low = (incoming - high.astype(F32)).astype(BF16)
            q = query[rows, columns]
            carried = jnp.dot(q, high, preferred_element_type=F32)
            carried = carried + jnp.dot(q, low, preferred_element_type=F32)
            scale = jnp.where(inside, decay_of(decay[h], local + 1), 0.0)
            attn = inner[rows, columns] + carried * scale
            attn_out[rows, columns] = attn
            total = total + attn * attn
        line = jnp.sum(jnp.transpose(total), axis=0, keepdims=True)
        for i in range(BLOCK // HEAD):
            squares_out[pl.ds(s * (BLOCK // HEAD) + i, 1), :] = line[:, i * HEAD : (i + 1) * HEAD]


def combine(scan, scalars, query, inner, arrived, first_seq):
    rows = query.shape[0]
    return pl.pallas_call(
        functools.partial(combine_kernel, scan, first_seq),
        out_shape=[
            pltpu.VMEM((rows, WIDTH), F32),
            jax.ShapeDtypeStruct((rows // HEAD, HEAD), F32),
        ],
        in_specs=[SMEM] * 3 + [VMEM] * (2 + len(arrived)),
        out_specs=[VMEM] * 2,
        compiler_params=pltpu.CompilerParams(vmem_limit_bytes=LIMIT * 2**20),
        name="combine",
    )(*scalars, query, inner, *arrived)


def finish_kernel(width_all, attn_y, attn_z, gate_y, gate_z, squares, out):
    attns, gates = (attn_y, attn_z), (gate_y, gate_z)
    half = out.shape[0] // 2
    per = BLOCK // HEAD
    scales = lax.rsqrt(squares[...] * (1.0 / width_all) + EPSILON)
    for i in range(scales.shape[0]):
        scale = jnp.transpose(jnp.broadcast_to(scales[i : i + 1, :], (HEAD, HEAD)))
        s, r = i // per, i % per
        rows = pl.ds((s % half) * BLOCK + r * HEAD, HEAD)
        for h in range(WIDTH // HEAD):
            columns = pl.ds(h * HEAD, HEAD)
            got = attns[s // half][rows, columns] * scale * gates[s // half][rows, columns]
            out[s, pl.ds(r * HEAD, HEAD), columns] = got.astype(BF16)


def finish(attns, gates, squares):
    width_all = WIDTH * lax.axis_size("tp")
    seqs = 2 * attns[0].shape[0] // BLOCK
    return pl.pallas_call(
        functools.partial(finish_kernel, width_all),
        out_shape=jax.ShapeDtypeStruct((seqs, BLOCK, WIDTH), BF16),
        in_specs=[VMEM] * 5,
        out_specs=VMEM,
        compiler_params=pltpu.CompilerParams(vmem_limit_bytes=LIMIT * 2**20),
        name="finish",
    )(*attns, *gates, squares)


def stack_kernel(first, second, out, sems):
    copies = [pltpu.make_async_copy(x, out.at[i], sems.at[i]) for i, x in enumerate((first, second))]
    for copy in copies:
        copy.start()
    for copy in copies:
        copy.wait()


def stack(first, second):
    return pl.pallas_call(
        stack_kernel,
        out_shape=pltpu.HBM((2, *first.shape), first.dtype),
        in_specs=[ANY] * 2,
        out_specs=HBM,
        scratch_shapes=[pltpu.SemaphoreType.DMA((2,))],
        compiler_params=pltpu.CompilerParams(vmem_limit_bytes=2**20),
        name="stack",
    )(first, second)


def add_kernel(first, second, out):
    out[...] = first[...] + second[...]


def add(first, second):
    return pl.pallas_call(
        add_kernel,
        out_shape=jax.ShapeDtypeStruct(first.shape, first.dtype),
        in_specs=[VMEM] * 2,
        out_specs=VMEM,
        compiler_params=pltpu.CompilerParams(vmem_limit_bytes=2**20),
        name="add",
    )(first, second)


def join_kernel(first, second, out):
    half = first.shape[0]
    out[pl.ds(0, half), :] = first[...]
    out[pl.ds(half, half), :] = second[...]


def join(first, second):
    return pl.pallas_call(
        join_kernel,
        out_shape=jax.ShapeDtypeStruct((2 * first.shape[0], first.shape[1]), first.dtype),
        in_specs=[VMEM] * 2,
        out_specs=VMEM,
        compiler_params=pltpu.CompilerParams(vmem_limit_bytes=2**20),
        name="join",
    )(first, second)


def all_sum(x):
    for route in (CORE, ACROSS, PAIR_A, PAIR_B):
        x = add(x, lax.ppermute(x, "tp", route))
    return x


def in_order(*groups):
    return lax.optimization_barrier(groups)


def on_device(hidden, w_query, w_key, w_value, w_gate, decay_rate, norm_gain, doc_lengths):
    seqs = hidden.shape[0]
    me = lax.axis_index("tp")
    my_y, my_z, my_c = me // 8, (me // 2) % 4, me % 2
    meta = [lax.axis_index("ctx") * BLOCK]
    gain = norm_gain.reshape(1, WIDTH)
    for flip, j in PIECES:
        for core in (0, 1):
            c = (my_c + core) % 2
            z = (my_z + j * (2 * c - 1) + 4) % 4
            meta.append((my_y + flip) % 2 * 8 + z * 2 + c)
    meta.append(lax.axis_index("ctx"))
    scalars = (jnp.stack(meta), doc_lengths, decay_rate)
    half = seqs // 2
    rows = hidden.reshape(seqs * BLOCK, SHARD)
    part_y, part_z = rows[: half * BLOCK], rows[half * BLOCK :]
    weights = [w_key, w_value, w_query, w_gate]
    held = {}

    def at(flip, j):
        return PIECES.index((flip, j))

    def one(x, flip, j):
        return [((x, other_core(x), None), at(flip, j))]

    def two(x, j):
        other = other_core(x)
        return [((x, other, flip), at(flip, j)) for flip in (0, 1)]

    y0, r1 = across(part_y), ring(part_z)
    rows_other = other_core(rows)
    own_y, own_z = [
        ((rows, rows_other, pl.ds(p * half * BLOCK, half * BLOCK)), at(0, 0)) for p in (0, 1)
    ]
    acc = project("first", scalars, [[own_y]], held, weights, [0, 1])
    acc, y0, r1, part_z = in_order(acc, y0, r1, part_z)

    a1, r2, far_a = ring(stack(part_y, y0)), ring(r1), across(stack(part_z, r1))
    parts = [one(y0, 1, 0), [own_z] + one(r1, 0, 1)]
    acc = project("more", scalars, parts, held, weights, [2, 3, 4], acc)
    acc, a1, r2, far_a = in_order(acc, a1, r2, far_a)

    a2, r3, far2 = ring(a1), ring(r2), across(r2)
    parts = [two(a1, 1), one(r2, 0, 2) + [(x, at(1, i)) for i, (x, _) in enumerate(two(far_a, 0))]]
    acc = project("more", scalars, parts, held, weights, [5, 6], acc)
    acc, a2, r3, far2 = in_order(acc, a2, r3, far2)

    a3, far3 = ring(a2), across(r3)
    parts = [two(a2, 2), one(r3, 0, 3) + one(far2, 1, 2)]
    acc = project("more", scalars, parts, held, weights, [7], acc)
    acc, a3, far3 = in_order(acc, a3, far3)

    last_y, last_z = [two(a3, 3)], [one(far3, 1, 3)]
    keys_y, values_y, state_y, sent_y = project("kv", scalars, last_y, held, accs=acc[:2])
    one_y = swapped(sent_y, 1)
    acc, state_y = in_order(acc, state_y)
    keys_z, values_z, state_z, sent_z = project(
        "kv", scalars, last_z, held, accs=acc[4:6], first_seq=half
    )
    above_z = ahead(sent_z, 4)
    acc, state_z = in_order(acc, state_z)
    query_y, inner_y, gate_y = project(
        "qg", scalars, last_y, held, accs=acc[2:4], extra=(keys_y, values_y, gain)
    )
    query_y, one_y, acc = in_order(query_y, one_y, acc)
    pair_y = extend(pair_kernel, scalars, state_y, one_y, 0)
    two_y = swapped(pair_y, 2)
    above_z, pair_y = in_order(above_z, pair_y)
    chosen = choose(scalars, sent_z, above_z)
    around_z = [round_x(x, distance) for distance, x in enumerate(chosen, 1)]
    acc, chosen = in_order(acc, chosen)
    query_z, inner_z, gate_z = project(
        "qg", scalars, last_z, held, accs=acc[6:], extra=(keys_z, values_z, gain), first_seq=half
    )
    query_z, two_y = in_order(query_z, two_y)
    four_y = ahead(extend(quad_kernel, scalars, pair_y, two_y, 0), 4)
    query_z, around_z = in_order(query_z, around_z)
    attn_z, squares_z = combine(False, scalars, query_z, inner_z, (*around_z, above_z), half)
    squares_z, four_y = in_order(squares_z, four_y)
    attn_y, squares_y = combine(True, scalars, query_y, inner_y, (one_y, two_y, four_y), 0)
    squares = all_sum(join(squares_y, squares_z))
    return finish((attn_y, attn_z), (gate_y, gate_z), squares)


def solution(mesh):
    in_specs = (
        P(None, "ctx", "tp"),
        P(None, "tp"),
        P(None, "tp"),
        P(None, "tp"),
        P(None, "tp"),
        P("tp"),
        P("tp"),
        P(),
    )
    out_specs = P(None, "ctx", "tp")
    return jax.shard_map(
        on_device, mesh=mesh, in_specs=in_specs, out_specs=out_specs, check_vma=False
    )
```

```python
import functools

import jax
import jax.numpy as jnp
from jax import lax
from jax.experimental import pallas as pl
from jax.experimental.pallas import tpu as pltpu
from jax.sharding import PartitionSpec as P

EPSILON = 1e-06
BLOCK = 256
HEAD = 128
SHARD = 384
WIDTH = 512
LIMIT = 16
F32 = jnp.float32
BF16 = jnp.bfloat16
ANY = pl.BlockSpec(memory_space=pl.ANY)
HBM = pl.BlockSpec(memory_space=pltpu.HBM)
SMEM = pl.BlockSpec(memory_space=pltpu.SMEM)
VMEM = pl.BlockSpec(memory_space=pltpu.VMEM)
PIECES = [(0, 0), (1, 0), (0, 1), (0, 2), (1, 1), (0, 3), (1, 2), (1, 3)]
PIECE = 2 * SHARD
CTX = 1 + 2 * len(PIECES)


def tp_route(step):
    route = []
    for y in range(2):
        for z in range(4):
            for c in range(2):
                y2, z2, c2 = step(y, z, c)
                route.append((y * 8 + z * 2 + c, (y2 % 2) * 8 + (z2 % 4) * 2 + c2 % 2))
    return route


RING = tp_route(lambda y, z, c: (y, z + 1 - 2 * c, c))
ACROSS = tp_route(lambda y, z, c: (y + 1, z, c))
CORE = tp_route(lambda y, z, c: (y, z, c + 1))
PAIR_A = tp_route(lambda y, z, c: (y, z ^ 1, c))
PAIR_B = tp_route(lambda y, z, c: (y, 3 - z, c))


def ring(x):
    return lax.ppermute(x, "tp", RING)


def across(x):
    return lax.ppermute(x, "tp", ACROSS)


def other_core(x):
    return lax.ppermute(x, "tp", CORE)


def ahead(x, distance):
    n = lax.axis_size("ctx")
    return lax.ppermute(x, "ctx", [(i, i + distance) for i in range(n - distance)])


def swapped(x, bit):
    return lax.ppermute(x, "ctx", [(i, i ^ bit) for i in range(lax.axis_size("ctx"))])


def round_x(x, distance):
    n = lax.axis_size("ctx")
    return lax.ppermute(x, "ctx", [(i, i // 4 * 4 + (i + distance) % 4) for i in range(n)])


def doc_ends(lengths, seq):
    first = lengths[seq, 0]
    second = first + lengths[seq, 1]
    return first, second, second + lengths[seq, 2]


def doc_of(position, ends):
    return sum((position >= end).astype(jnp.int32) for end in ends)


def decay_of(rate, steps):
    return jnp.exp(-rate * steps.astype(F32))


def project_kernel(mode, first_seq, plan, *refs):
    n_x, parts, loads, n_held, n_w, n_acc = plan
    refs = list(refs)
    take = lambda n: [refs.pop(0) for _ in range(n)]
    meta, lengths, decay = take(3) if mode in ("kv", "qg") else (take(1)[0], None, None)
    xs = take(n_x)
    held = take(n_held)
    weights = take(4) if loads else []
    accs = take(n_acc)
    if mode == "qg":
        k_in, v_in, gain = take(3)
    outs = take({"first": 4, "more": len(parts) * 4, "kv": 3, "qg": 3}[mode])
    loaded = take(len(loads))
    xbuf, xsem, wsem = take(3)
    held = held + loaded

    def x_copies(p, i):
        return [
            pltpu.make_async_copy(
                xs[array] if index is None else xs[array].at[index],
                xbuf.at[p, :, pl.ds((2 * i + core) * SHARD, SHARD)],
                xsem.at[p, 2 * i + core],
            )
            for core, (array, index) in enumerate(parts[p][i][0])
        ]

    def w_copies(i, n):
        return [
            pltpu.make_async_copy(
                weights[n].at[pl.ds(pl.multiple_of(meta[1 + 2 * loads[i] + core] * SHARD, SHARD), SHARD), :],
                loaded[i].at[n, pl.ds(core * SHARD, SHARD), :],
                wsem.at[i, n, core],
            )
            for core in (0, 1)
        ]

    order = [(p, i) for p in range(len(parts)) for i in range(len(parts[p]))]

    def start_x(chosen):
        for p, i in chosen:
            for copy in x_copies(p, i):
                copy.start()

    start_x(order[:2])
    def start_loads(chosen):
        for i in chosen:
            for n in range(4):
                for copy in w_copies(i, n):
                    copy.start()

    now = len({w for pieces in parts for _, w in pieces if w >= n_held})
    waited = set()
    start_loads(range(now))

    def load(i, n):
        if i >= 0 and (i, n) not in waited:
            waited.add((i, n))
            for copy in w_copies(i, n):
                copy.wait()

    def product(p, n, acc):
        total = None if acc is None else acc[...]
        for i, (_, w) in enumerate(parts[p]):
            if n in (0, 2 if mode == "qg" else 0):
                for copy in x_copies(p, i):
                    copy.wait()
                k = order.index((p, i)) + 2
                start_x(order[k : k + 1])
                if k == max(2, len(order) - 1):
                    start_loads(range(now, len(loads)))
            load(w - n_held, n)
            got = jnp.dot(
                xbuf[p, :, pl.ds(i * PIECE, PIECE)], held[w][n], preferred_element_type=F32
            )
            total = got if total is None else total + got
        return total

    offset = meta[0]

    def part(s, h):
        return pl.ds(s * BLOCK, BLOCK), pl.ds(h * HEAD, HEAD)

    heads = WIDTH // HEAD
    if mode == "first":
        for n in range(4):
            outs[n][...] = product(0, n, None)
    if mode == "more":
        for p in range(len(parts)):
            for n in range(4):
                k = 4 * p + n
                outs[k][...] = product(p, n, accs[k] if k < n_acc else None)
    if mode == "kv":
        k_out, v_out, s_out = outs
        k_out[...] = jax.nn.silu(product(0, 0, accs[0])).astype(BF16)
        v_out[...] = jax.nn.silu(product(0, 1, accs[1])).astype(BF16)
        local = lax.broadcasted_iota(jnp.int32, (BLOCK, HEAD), 0)
        for s in range(s_out.shape[0]):
            ends = doc_ends(lengths, first_seq + s)
            keep = doc_of(local + offset, ends) == doc_of(offset + BLOCK - 1, ends)
            for h in range(heads):
                scale = jnp.where(keep, decay_of(decay[h], BLOCK - 1 - local), 0.0)
                weighted = (k_out[part(s, h)].astype(F32) * scale).astype(BF16)
                state = lax.dot_general(
                    weighted, v_out[part(s, h)], (((0,), (0,)), ((), ())), preferred_element_type=F32
                )
                s_out[s, h] = state.astype(BF16)
    if mode == "qg":
        q_out, inner_out, gate_out = outs
        q_out[...] = jax.nn.silu(product(0, 2, accs[0])).astype(BF16)
        gate_out[...] = gain[...] * jax.nn.sigmoid(product(0, 3, accs[1]))
        row = lax.broadcasted_iota(jnp.int32, (BLOCK, BLOCK), 0)
        column = lax.broadcasted_iota(jnp.int32, (BLOCK, BLOCK), 1)
        causal = row >= column
        for h in range(heads):
            pair_decay = decay_of(decay[h], jnp.maximum(row - column, 0))
            for s in range(q_out.shape[0] // BLOCK):
                ends = doc_ends(lengths, first_seq + s)
                same = doc_of(row + offset, ends) == doc_of(column + offset, ends)
                scores = lax.dot_general(
                    q_out[part(s, h)],
                    k_in[part(s, h)],
                    (((1,), (1,)), ((), ())),
                    preferred_element_type=F32,
                )
                allowed = jnp.logical_and(causal, same)
                mixed = jnp.where(allowed, scores * pair_decay, 0.0).astype(BF16)
                inner_out[part(s, h)] = jnp.dot(
                    mixed, v_in[part(s, h)], preferred_element_type=F32
                )
    for i in range(len(loads)):
        for n in range(4):
            load(i, n)


def project(mode, scalars, parts, held, weights=(), loads=(), accs=(), extra=(), first_seq=0):
    arrays, plan_parts, used = [], [], []
    for pieces in parts:
        plan = []
        for (mine, other, index), number in pieces:
            for x in (mine, other):
                if all(x is not y for y in arrays):
                    arrays.append(x)
            where = [
                ([x is y for y in arrays].index(True), index) for x in (mine, other)
            ]
            if number in held and number not in used:
                used.append(number)
            plan.append((where, number))
        plan_parts.append(plan)
    numbers = used + list(loads)
    plan_parts = [[(where, numbers.index(number)) for where, number in plan] for plan in plan_parts]
    index = parts[0][0][0][2]
    rows = index.size if isinstance(index, pl.Slice) else arrays[0].shape[-2]
    half = jax.ShapeDtypeStruct((rows, WIDTH), BF16)
    wide = pltpu.VMEM((rows, WIDTH), F32)
    state = jax.ShapeDtypeStruct((rows // BLOCK, WIDTH // HEAD, HEAD, HEAD), BF16)
    outs = {
        "first": [wide] * 4,
        "more": [wide] * (4 * len(parts)),
        "kv": [half, half, state],
        "qg": [half, wide, wide],
    }[mode]
    n_outs = len(outs)
    if mode in ("first", "more"):
        scalars = scalars[:1]
    outs = outs + [pltpu.VMEM((4, PIECE, WIDTH), BF16)] * len(loads)
    most = max(len(p) for p in plan_parts)
    if mode == "first":
        arrays = [pltpu.with_memory_space_constraint(x, pltpu.HBM) for x in arrays]
    loading = [pltpu.with_memory_space_constraint(w, pltpu.HBM) for w in weights] if loads else []
    before = len(scalars) + len(arrays) + len(used) + len(loading)
    aliases = {before + n: n for n in range(len(accs))} if mode == "more" else {}
    plan = (len(arrays), plan_parts, list(loads), len(used), 4, len(accs))
    got = pl.pallas_call(
        functools.partial(project_kernel, mode, first_seq, plan),
        out_shape=outs,
        in_specs=[SMEM] * len(scalars)
        + [HBM if mode == "first" else ANY] * len(arrays)
        + [VMEM] * len(used)
        + [HBM] * len(loading)
        + [VMEM] * (len(accs) + len(extra)),
        out_specs=[VMEM] * len(outs),
        scratch_shapes=[
            pltpu.VMEM((len(parts), rows, most * PIECE), BF16),
            pltpu.SemaphoreType.DMA((len(parts), 2 * most)),
            pltpu.SemaphoreType.DMA((max(1, len(loads)), 4, 2)),
        ],
        input_output_aliases=aliases,
        compiler_params=pltpu.CompilerParams(vmem_limit_bytes=LIMIT * 2**20),
        cost_estimate=pl.CostEstimate(
            flops=2 * rows * PIECE * sum(len(p) for p in parts) * (4 if mode in ("first", "more") else 2) * WIDTH,
            bytes_accessed=2 * rows * PIECE,
            transcendentals=0,
        ),
        name="project_" + mode,
    )(*scalars, *arrays, *[held[n] for n in used], *loading, *accs, *extra)
    held.update(zip(loads, got[n_outs:]))
    return got[:n_outs]


def carried_share(meta, lengths, decay, s, h, block):
    ends = doc_ends(lengths, s)
    start = meta[0] - block * BLOCK
    keep = doc_of(start + BLOCK - 1, ends) == doc_of(start - 1, ends)
    rate = jnp.full((8, HEAD), decay[h] * (-1.0 * BLOCK), F32)
    return jnp.where(keep, jnp.exp(rate), 0.0)[0:1, :]


def one_or(condition, share):
    return jnp.where(condition, 1.0, share)


def pair_kernel(first_seq, meta, lengths, decay, state, before, out):
    odd = meta[CTX] % 2 == 1
    for s in range(state.shape[0]):
        for h in range(state.shape[1]):
            share = functools.partial(carried_share, meta, lengths, decay, first_seq + s, h)
            mine, other = one_or(odd, share(-1)), one_or(jnp.logical_not(odd), share(0))
            got = mine * state[s, h].astype(F32) + other * before[s, h].astype(F32)
            out[s, h] = got.astype(BF16)


def quad_kernel(first_seq, meta, lengths, decay, state, before, out):
    odd, high = meta[CTX] % 2, meta[CTX] // 2 % 2 == 1
    for s in range(state.shape[0]):
        for h in range(state.shape[1]):
            share = functools.partial(carried_share, meta, lengths, decay, first_seq + s, h)
            mine = one_or(high, share(odd - 2) * share(odd - 3))
            other = one_or(jnp.logical_not(high), share(odd) * share(odd - 1))
            got = mine * state[s, h].astype(F32) + other * before[s, h].astype(F32)
            out[s, h] = got.astype(BF16)


def choose_kernel(meta, state, earlier, *outs):
    for distance, out in enumerate(outs, 1):
        wraps = meta[CTX] % 4 + distance >= 4
        for s in range(state.shape[0]):
            for h in range(state.shape[1]):
                out[s, h] = jnp.where(wraps, earlier[s, h], state[s, h])


def choose(scalars, state, earlier):
    return pl.pallas_call(
        choose_kernel,
        out_shape=[jax.ShapeDtypeStruct(state.shape, BF16)] * 3,
        in_specs=[SMEM] + [VMEM] * 2,
        out_specs=[VMEM] * 3,
        compiler_params=pltpu.CompilerParams(vmem_limit_bytes=LIMIT * 2**20),
        name="choose",
    )(scalars[0], state, earlier)


def extend(kernel, scalars, state, before, first_seq):
    return pl.pallas_call(
        functools.partial(kernel, first_seq),
        out_shape=jax.ShapeDtypeStruct(state.shape, BF16),
        in_specs=[SMEM] * 3 + [VMEM] * 2,
        out_specs=VMEM,
        compiler_params=pltpu.CompilerParams(vmem_limit_bytes=LIMIT * 2**20),
        name="extend",
    )(*scalars, state, before)


def shares(scan, meta, share):
    if not scan:
        return [1.0, share(1), share(1) * share(2), share(1) * share(2) * share(3)]
    place = meta[CTX] % 4
    odd, high = place % 2 == 1, place >= 2
    first = jnp.where(odd, 1.0, jnp.zeros((1, HEAD), F32))
    second = jnp.where(high, one_or(jnp.logical_not(odd), share(1)), 0.0)
    third = one_or(place < 1, share(1)) * one_or(place < 2, share(2)) * one_or(place < 3, share(3))
    return [first, second, third]


def combine_kernel(scan, first_seq, meta, lengths, decay, query, inner, *refs):
    arrived, (attn_out, squares_out) = refs[:-2], refs[-2:]
    seqs, heads = arrived[0].shape[:2]
    offset = meta[0]
    local = lax.broadcasted_iota(jnp.int32, (BLOCK, HEAD), 0)
    for s in range(seqs):
        ends = doc_ends(lengths, first_seq + s)
        inside = doc_of(local + offset, ends) == doc_of(offset - 1, ends)
        total = jnp.zeros((BLOCK, HEAD), F32)
        rows = pl.ds(s * BLOCK, BLOCK)
        for h in range(heads):
            columns = pl.ds(h * HEAD, HEAD)
            share = functools.partial(carried_share, meta, lengths, decay, first_seq + s, h)
            incoming = sum(
                weight * x[s, h].astype(F32) for weight, x in zip(shares(scan, meta, share), arrived)
            )
            high = incoming.astype(BF16)
            low = (incoming - high.astype(F32)).astype(BF16)
            q = query[rows, columns]
            carried = jnp.dot(q, high, preferred_element_type=F32)
            carried = carried + jnp.dot(q, low, preferred_element_type=F32)
            scale = jnp.where(inside, decay_of(decay[h], local + 1), 0.0)
            attn = inner[rows, columns] + carried * scale
            attn_out[rows, columns] = attn
            total = total + attn * attn
        line = jnp.sum(jnp.transpose(total), axis=0, keepdims=True)
        for i in range(BLOCK // HEAD):
            squares_out[pl.ds(s * (BLOCK // HEAD) + i, 1), :] = line[:, i * HEAD : (i + 1) * HEAD]


def combine(scan, scalars, query, inner, arrived, first_seq):
    rows = query.shape[0]
    return pl.pallas_call(
        functools.partial(combine_kernel, scan, first_seq),
        out_shape=[
            pltpu.VMEM((rows, WIDTH), F32),
            jax.ShapeDtypeStruct((rows // HEAD, HEAD), F32),
        ],
        in_specs=[SMEM] * 3 + [VMEM] * (2 + len(arrived)),
        out_specs=[VMEM] * 2,
        compiler_params=pltpu.CompilerParams(vmem_limit_bytes=LIMIT * 2**20),
        name="combine",
    )(*scalars, query, inner, *arrived)


def finish_kernel(width_all, attn_y, attn_z, gate_y, gate_z, squares, out):
    attns, gates = (attn_y, attn_z), (gate_y, gate_z)
    half = out.shape[0] // 2
    per = BLOCK // HEAD
    scales = lax.rsqrt(squares[...] * (1.0 / width_all) + EPSILON)
    for i in range(scales.shape[0]):
        scale = jnp.transpose(jnp.broadcast_to(scales[i : i + 1, :], (HEAD, HEAD)))
        s, r = i // per, i % per
        rows = pl.ds((s % half) * BLOCK + r * HEAD, HEAD)
        for h in range(WIDTH // HEAD):
            columns = pl.ds(h * HEAD, HEAD)
            got = attns[s // half][rows, columns] * scale * gates[s // half][rows, columns]
            out[s, pl.ds(r * HEAD, HEAD), columns] = got.astype(BF16)


def finish(attns, gates, squares):
    width_all = WIDTH * lax.axis_size("tp")
    seqs = 2 * attns[0].shape[0] // BLOCK
    return pl.pallas_call(
        functools.partial(finish_kernel, width_all),
        out_shape=jax.ShapeDtypeStruct((seqs, BLOCK, WIDTH), BF16),
        in_specs=[VMEM] * 5,
        out_specs=VMEM,
        compiler_params=pltpu.CompilerParams(vmem_limit_bytes=LIMIT * 2**20),
        name="finish",
    )(*attns, *gates, squares)


def stack_kernel(first, second, out, sems):
    copies = [pltpu.make_async_copy(x, out.at[i], sems.at[i]) for i, x in enumerate((first, second))]
    for copy in copies:
        copy.start()
    for copy in copies:
        copy.wait()


def stack(first, second):
    return pl.pallas_call(
        stack_kernel,
        out_shape=pltpu.HBM((2, *first.shape), first.dtype),
        in_specs=[ANY] * 2,
        out_specs=HBM,
        scratch_shapes=[pltpu.SemaphoreType.DMA((2,))],
        compiler_params=pltpu.CompilerParams(vmem_limit_bytes=2**20),
        name="stack",
    )(first, second)


def add_kernel(first, second, out):
    out[...] = first[...] + second[...]


def add(first, second):
    return pl.pallas_call(
        add_kernel,
        out_shape=jax.ShapeDtypeStruct(first.shape, first.dtype),
        in_specs=[VMEM] * 2,
        out_specs=VMEM,
        compiler_params=pltpu.CompilerParams(vmem_limit_bytes=2**20),
        name="add",
    )(first, second)


def join_kernel(first, second, out):
    half = first.shape[0]
    out[pl.ds(0, half), :] = first[...]
    out[pl.ds(half, half), :] = second[...]


def join(first, second):
    return pl.pallas_call(
        join_kernel,
        out_shape=jax.ShapeDtypeStruct((2 * first.shape[0], first.shape[1]), first.dtype),
        in_specs=[VMEM] * 2,
        out_specs=VMEM,
        compiler_params=pltpu.CompilerParams(vmem_limit_bytes=2**20),
        name="join",
    )(first, second)


def all_sum(x):
    for route in (CORE, ACROSS, PAIR_A, PAIR_B):
        x = add(x, lax.ppermute(x, "tp", route))
    return x


def in_order(*groups):
    return lax.optimization_barrier(groups)


def on_device(hidden, w_query, w_key, w_value, w_gate, decay_rate, norm_gain, doc_lengths):
    seqs = hidden.shape[0]
    me = lax.axis_index("tp")
    my_y, my_z, my_c = me // 8, (me // 2) % 4, me % 2
    meta = [lax.axis_index("ctx") * BLOCK]
    gain = norm_gain.reshape(1, WIDTH)
    for flip, j in PIECES:
        for core in (0, 1):
            c = (my_c + core) % 2
            z = (my_z + j * (2 * c - 1) + 4) % 4
            meta.append((my_y + flip) % 2 * 8 + z * 2 + c)
    meta.append(lax.axis_index("ctx"))
    scalars = (jnp.stack(meta), doc_lengths, decay_rate)
    half = seqs // 2
    rows = hidden.reshape(seqs * BLOCK, SHARD)
    part_y, part_z = rows[: half * BLOCK], rows[half * BLOCK :]
    weights = [w_key, w_value, w_query, w_gate]
    held = {}

    def at(flip, j):
        return PIECES.index((flip, j))

    def one(x, flip, j):
        return [((x, other_core(x), None), at(flip, j))]

    def two(x, j):
        other = other_core(x)
        return [((x, other, flip), at(flip, j)) for flip in (0, 1)]

    y0, r1 = across(part_y), ring(part_z)
    rows_other = other_core(rows)
    own_y, own_z = [
        ((rows, rows_other, pl.ds(p * half * BLOCK, half * BLOCK)), at(0, 0)) for p in (0, 1)
    ]
    acc = project("first", scalars, [[own_y]], held, weights, [0, 1])
    acc, y0, r1, part_z = in_order(acc, y0, r1, part_z)

    a1, r2, far_a = ring(stack(part_y, y0)), ring(r1), across(stack(part_z, r1))
    parts = [one(y0, 1, 0), [own_z] + one(r1, 0, 1)]
    acc = project("more", scalars, parts, held, weights, [2, 3, 4], acc)
    acc, a1, r2, far_a = in_order(acc, a1, r2, far_a)

    a2, r3, far2 = ring(a1), ring(r2), across(r2)
    parts = [two(a1, 1), one(r2, 0, 2) + [(x, at(1, i)) for i, (x, _) in enumerate(two(far_a, 0))]]
    acc = project("more", scalars, parts, held, weights, [5, 6], acc)
    acc, a2, r3, far2 = in_order(acc, a2, r3, far2)

    a3, far3 = ring(a2), across(r3)
    parts = [two(a2, 2), one(r3, 0, 3) + one(far2, 1, 2)]
    acc = project("more", scalars, parts, held, weights, [7], acc)
    acc, a3, far3 = in_order(acc, a3, far3)

    last_y, last_z = [two(a3, 3)], [one(far3, 1, 3)]
    keys_y, values_y, sent_y = project("kv", scalars, last_y, held, accs=acc[:2])
    one_y = swapped(sent_y, 1)
    acc, state_y = in_order(acc, sent_y)
    keys_z, values_z, sent_z = project(
        "kv", scalars, last_z, held, accs=acc[4:6], first_seq=half
    )
    above_z = ahead(sent_z, 4)
    acc, state_z = in_order(acc, sent_z)
    query_y, inner_y, gate_y = project(
        "qg", scalars, last_y, held, accs=acc[2:4], extra=(keys_y, values_y, gain)
    )
    query_y, one_y, acc = in_order(query_y, one_y, acc)
    pair_y = extend(pair_kernel, scalars, state_y, one_y, 0)
    two_y = swapped(pair_y, 2)
    above_z, pair_y = in_order(above_z, pair_y)
    chosen = choose(scalars, state_z, above_z)
    around_z = [round_x(x, distance) for distance, x in enumerate(chosen, 1)]
    acc, chosen = in_order(acc, chosen)
    query_z, inner_z, gate_z = project(
        "qg", scalars, last_z, held, accs=acc[6:], extra=(keys_z, values_z, gain), first_seq=half
    )
    query_z, two_y = in_order(query_z, two_y)
    four_y = ahead(extend(quad_kernel, scalars, pair_y, two_y, 0), 4)
    query_z, around_z = in_order(query_z, around_z)
    attn_z, squares_z = combine(False, scalars, query_z, inner_z, (*around_z, above_z), half)
    squares_z, four_y = in_order(squares_z, four_y)
    attn_y, squares_y = combine(True, scalars, query_y, inner_y, (one_y, two_y, four_y), 0)
    squares = all_sum(join(squares_y, squares_z))
    return finish((attn_y, attn_z), (gate_y, gate_z), squares)


def solution(mesh):
    in_specs = (
        P(None, "ctx", "tp"),
        P(None, "tp"),
        P(None, "tp"),
        P(None, "tp"),
        P(None, "tp"),
        P("tp"),
        P("tp"),
        P(),
    )
    out_specs = P(None, "ctx", "tp")
    return jax.shard_map(
        on_device, mesh=mesh, in_specs=in_specs, out_specs=out_specs, check_vma=False
    )
```

```python
import functools

import jax
import jax.numpy as jnp
from jax import lax
from jax.experimental import pallas as pl
from jax.experimental.pallas import tpu as pltpu
from jax.sharding import PartitionSpec as P

EPSILON = 1e-06
BLOCK = 256
HEAD = 128
SHARD = 384
WIDTH = 512
LIMIT = 16
F32 = jnp.float32
BF16 = jnp.bfloat16
ANY = pl.BlockSpec(memory_space=pl.ANY)
HBM = pl.BlockSpec(memory_space=pltpu.HBM)
SMEM = pl.BlockSpec(memory_space=pltpu.SMEM)
VMEM = pl.BlockSpec(memory_space=pltpu.VMEM)
PIECES = [(0, 0), (1, 0), (0, 1), (0, 2), (1, 1), (0, 3), (1, 2), (1, 3)]
PIECE = 2 * SHARD
CTX = 1 + 2 * len(PIECES)


def tp_route(step):
    route = []
    for y in range(2):
        for z in range(4):
            for c in range(2):
                y2, z2, c2 = step(y, z, c)
                route.append((y * 8 + z * 2 + c, (y2 % 2) * 8 + (z2 % 4) * 2 + c2 % 2))
    return route


RING = tp_route(lambda y, z, c: (y, z + 1 - 2 * c, c))
ACROSS = tp_route(lambda y, z, c: (y + 1, z, c))
CORE = tp_route(lambda y, z, c: (y, z, c + 1))
PAIR_A = tp_route(lambda y, z, c: (y, z ^ 1, c))
PAIR_B = tp_route(lambda y, z, c: (y, 3 - z, c))


def ring(x):
    return lax.ppermute(x, "tp", RING)


def across(x):
    return lax.ppermute(x, "tp", ACROSS)


def other_core(x):
    return lax.ppermute(x, "tp", CORE)


def ahead(x, distance):
    n = lax.axis_size("ctx")
    return lax.ppermute(x, "ctx", [(i, i + distance) for i in range(n - distance)])


def swapped(x, bit):
    return lax.ppermute(x, "ctx", [(i, i ^ bit) for i in range(lax.axis_size("ctx"))])


def round_x(x, distance):
    n = lax.axis_size("ctx")
    return lax.ppermute(x, "ctx", [(i, i // 4 * 4 + (i + distance) % 4) for i in range(n)])


def doc_ends(lengths, seq):
    first = lengths[seq, 0]
    second = first + lengths[seq, 1]
    return first, second, second + lengths[seq, 2]


def doc_of(position, ends):
    return sum((position >= end).astype(jnp.int32) for end in ends)


def decay_of(rate, steps):
    return jnp.exp(-rate * steps.astype(F32))


def project_kernel(mode, first_seq, plan, *refs):
    n_x, parts, loads, n_held, n_w, n_acc = plan
    refs = list(refs)
    take = lambda n: [refs.pop(0) for _ in range(n)]
    meta, lengths, decay = take(3) if mode in ("kv", "qg") else (take(1)[0], None, None)
    xs = take(n_x)
    held = take(n_held)
    weights = take(4) if loads else []
    accs = take(n_acc)
    if mode == "qg":
        k_in, v_in, gain = take(3)
    outs = take({"first": 4, "more": len(parts) * 4, "kv": 3, "qg": 3}[mode])
    loaded = take(len(loads))
    xbuf, xsem, wsem = take(3)
    held = held + loaded

    def x_copies(p, i):
        return [
            pltpu.make_async_copy(
                xs[array] if index is None else xs[array].at[index],
                xbuf.at[p, :, pl.ds((2 * i + core) * SHARD, SHARD)],
                xsem.at[p, 2 * i + core],
            )
            for core, (array, index) in enumerate(parts[p][i][0])
        ]

    def w_copies(i, n):
        return [
            pltpu.make_async_copy(
                weights[n].at[pl.ds(pl.multiple_of(meta[1 + 2 * loads[i] + core] * SHARD, SHARD), SHARD), :],
                loaded[i].at[n, pl.ds(core * SHARD, SHARD), :],
                wsem.at[i, n, core],
            )
            for core in (0, 1)
        ]

    order = [(p, i) for p in range(len(parts)) for i in range(len(parts[p]))]

    def start_x(chosen):
        for p, i in chosen:
            for copy in x_copies(p, i):
                copy.start()

    start_x(order[:2])
    def start_loads(chosen):
        for i in chosen:
            for n in range(4):
                for copy in w_copies(i, n):
                    copy.start()

    now = len({w for pieces in parts for _, w in pieces if w >= n_held})
    waited = set()
    start_loads(range(now))

    def load(i, n):
        if i >= 0 and (i, n) not in waited:
            waited.add((i, n))
            for copy in w_copies(i, n):
                copy.wait()

    def product(p, n, acc):
        total = None if acc is None else acc[...]
        for i, (_, w) in enumerate(parts[p]):
            if n in (0, 2 if mode == "qg" else 0):
                for copy in x_copies(p, i):
                    copy.wait()
                k = order.index((p, i)) + 2
                start_x(order[k : k + 1])
                if k == max(2, len(order) - 1):
                    start_loads(range(now, len(loads)))
            load(w - n_held, n)
            got = jnp.dot(
                xbuf[p, :, pl.ds(i * PIECE, PIECE)], held[w][n], preferred_element_type=F32
            )
            total = got if total is None else total + got
        return total

    offset = meta[0]

    def part(s, h):
        return pl.ds(s * BLOCK, BLOCK), pl.ds(h * HEAD, HEAD)

    heads = WIDTH // HEAD
    if mode == "first":
        for n in range(4):
            outs[n][...] = product(0, n, None)
    if mode == "more":
        for p in range(len(parts)):
            for n in range(4):
                k = 4 * p + n
                outs[k][...] = product(p, n, accs[k] if k < n_acc else None)
    if mode == "kv":
        k_out, v_out, s_out = outs
        k_out[...] = jax.nn.silu(product(0, 0, accs[0])).astype(BF16)
        v_out[...] = jax.nn.silu(product(0, 1, accs[1])).astype(BF16)
        local = lax.broadcasted_iota(jnp.int32, (BLOCK, HEAD), 0)
        for s in range(s_out.shape[0]):
            ends = doc_ends(lengths, first_seq + s)
            keep = doc_of(local + offset, ends) == doc_of(offset + BLOCK - 1, ends)
            for h in range(heads):
                scale = jnp.where(keep, decay_of(decay[h], BLOCK - 1 - local), 0.0)
                weighted = (k_out[part(s, h)].astype(F32) * scale).astype(BF16)
                state = lax.dot_general(
                    weighted, v_out[part(s, h)], (((0,), (0,)), ((), ())), preferred_element_type=F32
                )
                s_out[s, h] = state.astype(BF16)
    if mode == "qg":
        q_out, inner_out, gate_out = outs
        q_out[...] = jax.nn.silu(product(0, 2, accs[0])).astype(BF16)
        gate_out[...] = gain[...] * jax.nn.sigmoid(product(0, 3, accs[1]))
        row = lax.broadcasted_iota(jnp.int32, (BLOCK, BLOCK), 0)
        column = lax.broadcasted_iota(jnp.int32, (BLOCK, BLOCK), 1)
        causal = row >= column
        for h in range(heads):
            pair_decay = decay_of(decay[h], jnp.maximum(row - column, 0))
            for s in range(q_out.shape[0] // BLOCK):
                ends = doc_ends(lengths, first_seq + s)
                same = doc_of(row + offset, ends) == doc_of(column + offset, ends)
                scores = lax.dot_general(
                    q_out[part(s, h)],
                    k_in[part(s, h)],
                    (((1,), (1,)), ((), ())),
                    preferred_element_type=F32,
                )
                allowed = jnp.logical_and(causal, same)
                mixed = jnp.where(allowed, scores * pair_decay, 0.0).astype(BF16)
                inner_out[part(s, h)] = jnp.dot(
                    mixed, v_in[part(s, h)], preferred_element_type=F32
                )
    for i in range(len(loads)):
        for n in range(4):
            load(i, n)


def project(mode, scalars, parts, held, weights=(), loads=(), accs=(), extra=(), first_seq=0):
    arrays, plan_parts, used = [], [], []
    for pieces in parts:
        plan = []
        for (mine, other, index), number in pieces:
            for x in (mine, other):
                if all(x is not y for y in arrays):
                    arrays.append(x)
            where = [
                ([x is y for y in arrays].index(True), index) for x in (mine, other)
            ]
            if number in held and number not in used:
                used.append(number)
            plan.append((where, number))
        plan_parts.append(plan)
    numbers = used + list(loads)
    plan_parts = [[(where, numbers.index(number)) for where, number in plan] for plan in plan_parts]
    index = parts[0][0][0][2]
    rows = index.size if isinstance(index, pl.Slice) else arrays[0].shape[-2]
    half = jax.ShapeDtypeStruct((rows, WIDTH), BF16)
    wide = pltpu.VMEM((rows, WIDTH), F32)
    state = jax.ShapeDtypeStruct((rows // BLOCK, WIDTH // HEAD, HEAD, HEAD), BF16)
    outs = {
        "first": [wide] * 4,
        "more": [wide] * (4 * len(parts)),
        "kv": [half, half, state],
        "qg": [half, wide, wide],
    }[mode]
    n_outs = len(outs)
    if mode in ("first", "more"):
        scalars = scalars[:1]
    outs = outs + [pltpu.VMEM((4, PIECE, WIDTH), BF16)] * len(loads)
    most = max(len(p) for p in plan_parts)
    if mode == "first":
        arrays = [pltpu.with_memory_space_constraint(x, pltpu.HBM) for x in arrays]
    loading = [pltpu.with_memory_space_constraint(w, pltpu.HBM) for w in weights] if loads else []
    before = len(scalars) + len(arrays) + len(used) + len(loading)
    aliases = {before + n: n for n in range(len(accs))} if mode == "more" else {}
    plan = (len(arrays), plan_parts, list(loads), len(used), 4, len(accs))
    got = pl.pallas_call(
        functools.partial(project_kernel, mode, first_seq, plan),
        out_shape=outs,
        in_specs=[SMEM] * len(scalars)
        + [HBM if mode == "first" else ANY] * len(arrays)
        + [VMEM] * len(used)
        + [HBM] * len(loading)
        + [VMEM] * (len(accs) + len(extra)),
        out_specs=[VMEM] * len(outs),
        scratch_shapes=[
            pltpu.VMEM((len(parts), rows, most * PIECE), BF16),
            pltpu.SemaphoreType.DMA((len(parts), 2 * most)),
            pltpu.SemaphoreType.DMA((max(1, len(loads)), 4, 2)),
        ],
        input_output_aliases=aliases,
        compiler_params=pltpu.CompilerParams(vmem_limit_bytes=LIMIT * 2**20),
        cost_estimate=pl.CostEstimate(
            flops=2 * rows * PIECE * sum(len(p) for p in parts) * (4 if mode in ("first", "more") else 2) * WIDTH,
            bytes_accessed=2 * rows * PIECE,
            transcendentals=0,
        ),
        name="project_" + mode,
    )(*scalars, *arrays, *[held[n] for n in used], *loading, *accs, *extra)
    held.update(zip(loads, got[n_outs:]))
    return got[:n_outs]


def carried_share(meta, lengths, decay, s, h, block):
    ends = doc_ends(lengths, s)
    start = meta[0] - block * BLOCK
    keep = doc_of(start + BLOCK - 1, ends) == doc_of(start - 1, ends)
    rate = jnp.full((8, HEAD), decay[h] * (-1.0 * BLOCK), F32)
    return jnp.where(keep, jnp.exp(rate), 0.0)[0:1, :]


def one_or(condition, share):
    return jnp.where(condition, 1.0, share)


def pair_kernel(first_seq, meta, lengths, decay, state, before, out):
    odd = meta[CTX] % 2 == 1
    for s in range(state.shape[0]):
        for h in range(state.shape[1]):
            share = functools.partial(carried_share, meta, lengths, decay, first_seq + s, h)
            mine, other = one_or(odd, share(-1)), one_or(jnp.logical_not(odd), share(0))
            got = mine * state[s, h].astype(F32) + other * before[s, h].astype(F32)
            out[s, h] = got.astype(BF16)


def quad_kernel(first_seq, meta, lengths, decay, state, before, out):
    odd, high = meta[CTX] % 2, meta[CTX] // 2 % 2 == 1
    for s in range(state.shape[0]):
        for h in range(state.shape[1]):
            share = functools.partial(carried_share, meta, lengths, decay, first_seq + s, h)
            mine = one_or(high, share(odd - 2) * share(odd - 3))
            other = one_or(jnp.logical_not(high), share(odd) * share(odd - 1))
            got = mine * state[s, h].astype(F32) + other * before[s, h].astype(F32)
            out[s, h] = got.astype(BF16)


def choose_kernel(meta, state, earlier, *outs):
    for distance, out in enumerate(outs, 1):
        wraps = meta[CTX] % 4 + distance >= 4
        for s in range(state.shape[0]):
            for h in range(state.shape[1]):
                out[s, h] = jnp.where(wraps, earlier[s, h], state[s, h])


def choose(scalars, state, earlier):
    return pl.pallas_call(
        choose_kernel,
        out_shape=[jax.ShapeDtypeStruct(state.shape, BF16)] * 3,
        in_specs=[SMEM] + [VMEM] * 2,
        out_specs=[VMEM] * 3,
        compiler_params=pltpu.CompilerParams(vmem_limit_bytes=LIMIT * 2**20),
        name="choose",
    )(scalars[0], state, earlier)


def extend(kernel, scalars, state, before, first_seq):
    return pl.pallas_call(
        functools.partial(kernel, first_seq),
        out_shape=jax.ShapeDtypeStruct(state.shape, BF16),
        in_specs=[SMEM] * 3 + [VMEM] * 2,
        out_specs=VMEM,
        compiler_params=pltpu.CompilerParams(vmem_limit_bytes=LIMIT * 2**20),
        name="extend",
    )(*scalars, state, before)


def shares(scan, meta, share):
    if not scan:
        return [1.0, share(1), share(1) * share(2), share(1) * share(2) * share(3)]
    place = meta[CTX] % 4
    odd, high = place % 2 == 1, place >= 2
    first = jnp.where(odd, 1.0, jnp.zeros((1, HEAD), F32))
    second = jnp.where(high, one_or(jnp.logical_not(odd), share(1)), 0.0)
    third = one_or(place < 1, share(1)) * one_or(place < 2, share(2)) * one_or(place < 3, share(3))
    return [first, second, third]


def combine_kernel(scan, first_seq, meta, lengths, decay, query, inner, *refs):
    arrived, (attn_out, squares_out) = refs[:-2], refs[-2:]
    seqs, heads = arrived[0].shape[:2]
    offset = meta[0]
    local = lax.broadcasted_iota(jnp.int32, (BLOCK, HEAD), 0)
    for s in range(seqs):
        ends = doc_ends(lengths, first_seq + s)
        inside = doc_of(local + offset, ends) == doc_of(offset - 1, ends)
        total = jnp.zeros((BLOCK, HEAD), F32)
        rows = pl.ds(s * BLOCK, BLOCK)
        for h in range(heads):
            columns = pl.ds(h * HEAD, HEAD)
            share = functools.partial(carried_share, meta, lengths, decay, first_seq + s, h)
            incoming = sum(
                weight * x[s, h].astype(F32) for weight, x in zip(shares(scan, meta, share), arrived)
            )
            high = incoming.astype(BF16)
            low = (incoming - high.astype(F32)).astype(BF16)
            q = query[rows, columns]
            carried = jnp.dot(q, high, preferred_element_type=F32)
            carried = carried + jnp.dot(q, low, preferred_element_type=F32)
            scale = jnp.where(inside, decay_of(decay[h], local + 1), 0.0)
            attn = inner[rows, columns] + carried * scale
            attn_out[rows, columns] = attn
            total = total + attn * attn
        line = jnp.sum(jnp.transpose(total), axis=0, keepdims=True)
        for i in range(BLOCK // HEAD):
            squares_out[pl.ds(s * (BLOCK // HEAD) + i, 1), :] = line[:, i * HEAD : (i + 1) * HEAD]


def combine(scan, scalars, query, inner, arrived, first_seq):
    rows = query.shape[0]
    return pl.pallas_call(
        functools.partial(combine_kernel, scan, first_seq),
        out_shape=[
            pltpu.VMEM((rows, WIDTH), F32),
            jax.ShapeDtypeStruct((rows // HEAD, HEAD), F32),
        ],
        in_specs=[SMEM] * 3 + [VMEM] * (2 + len(arrived)),
        out_specs=[VMEM] * 2,
        compiler_params=pltpu.CompilerParams(vmem_limit_bytes=LIMIT * 2**20),
        name="combine",
    )(*scalars, query, inner, *arrived)


def finish_kernel(width_all, attn_y, attn_z, gate_y, gate_z, squares, out):
    attns, gates = (attn_y, attn_z), (gate_y, gate_z)
    half = out.shape[0] // 2
    per = BLOCK // HEAD
    scales = lax.rsqrt(squares[...] * (1.0 / width_all) + EPSILON)
    for i in range(scales.shape[0]):
        scale = jnp.transpose(jnp.broadcast_to(scales[i : i + 1, :], (HEAD, HEAD)))
        s, r = i // per, i % per
        rows = pl.ds((s % half) * BLOCK + r * HEAD, HEAD)
        for h in range(WIDTH // HEAD):
            columns = pl.ds(h * HEAD, HEAD)
            got = attns[s // half][rows, columns] * scale * gates[s // half][rows, columns]
            out[s, pl.ds(r * HEAD, HEAD), columns] = got.astype(BF16)


def finish(attns, gates, squares):
    width_all = WIDTH * lax.axis_size("tp")
    seqs = 2 * attns[0].shape[0] // BLOCK
    return pl.pallas_call(
        functools.partial(finish_kernel, width_all),
        out_shape=jax.ShapeDtypeStruct((seqs, BLOCK, WIDTH), BF16),
        in_specs=[VMEM] * 5,
        out_specs=VMEM,
        compiler_params=pltpu.CompilerParams(vmem_limit_bytes=LIMIT * 2**20),
        name="finish",
    )(*attns, *gates, squares)


def stack_kernel(n, *refs):
    xs, outs, sems = refs[: 2 * n], refs[2 * n : 3 * n], refs[-1]
    copies = [
        pltpu.make_async_copy(x, outs[i // 2].at[i % 2], sems.at[i]) for i, x in enumerate(xs)
    ]
    for copy in copies:
        copy.start()
    for copy in copies:
        copy.wait()


def stack(*pairs):
    parts = [x for pair in pairs for x in pair]
    return pl.pallas_call(
        functools.partial(stack_kernel, len(pairs)),
        out_shape=[pltpu.HBM((2, *first.shape), first.dtype) for first, _ in pairs],
        in_specs=[ANY] * len(parts),
        out_specs=[HBM] * len(pairs),
        scratch_shapes=[pltpu.SemaphoreType.DMA((len(parts),))],
        compiler_params=pltpu.CompilerParams(vmem_limit_bytes=2**20),
        name="stack",
    )(*parts)


def add_kernel(first, second, out):
    out[...] = first[...] + second[...]


def add(first, second):
    return pl.pallas_call(
        add_kernel,
        out_shape=jax.ShapeDtypeStruct(first.shape, first.dtype),
        in_specs=[VMEM] * 2,
        out_specs=VMEM,
        compiler_params=pltpu.CompilerParams(vmem_limit_bytes=2**20),
        name="add",
    )(first, second)


def join_kernel(first, second, out):
    half = first.shape[0]
    out[pl.ds(0, half), :] = first[...]
    out[pl.ds(half, half), :] = second[...]


def join(first, second):
    return pl.pallas_call(
        join_kernel,
        out_shape=jax.ShapeDtypeStruct((2 * first.shape[0], first.shape[1]), first.dtype),
        in_specs=[VMEM] * 2,
        out_specs=VMEM,
        compiler_params=pltpu.CompilerParams(vmem_limit_bytes=2**20),
        name="join",
    )(first, second)


def all_sum(x):
    for route in (CORE, ACROSS, PAIR_A, PAIR_B):
        x = add(x, lax.ppermute(x, "tp", route))
    return x


def in_order(*groups):
    return lax.optimization_barrier(groups)


def on_device(hidden, w_query, w_key, w_value, w_gate, decay_rate, norm_gain, doc_lengths):
    seqs = hidden.shape[0]
    me = lax.axis_index("tp")
    my_y, my_z, my_c = me // 8, (me // 2) % 4, me % 2
    meta = [lax.axis_index("ctx") * BLOCK]
    gain = norm_gain.reshape(1, WIDTH)
    for flip, j in PIECES:
        for core in (0, 1):
            c = (my_c + core) % 2
            z = (my_z + j * (2 * c - 1) + 4) % 4
            meta.append((my_y + flip) % 2 * 8 + z * 2 + c)
    meta.append(lax.axis_index("ctx"))
    scalars = (jnp.stack(meta), doc_lengths, decay_rate)
    half = seqs // 2
    rows = hidden.reshape(seqs * BLOCK, SHARD)
    part_y, part_z = rows[: half * BLOCK], rows[half * BLOCK :]
    weights = [w_key, w_value, w_query, w_gate]
    held = {}

    def at(flip, j):
        return PIECES.index((flip, j))

    def one(x, flip, j):
        return [((x, other_core(x), None), at(flip, j))]

    def two(x, j):
        other = other_core(x)
        return [((x, other, flip), at(flip, j)) for flip in (0, 1)]

    y0, r1 = across(part_y), ring(part_z)
    rows_other = other_core(rows)
    own_y, own_z = [
        ((rows, rows_other, pl.ds(p * half * BLOCK, half * BLOCK)), at(0, 0)) for p in (0, 1)
    ]
    acc = project("first", scalars, [[own_y]], held, weights, [0, 1])
    acc, y0, r1, part_z = in_order(acc, y0, r1, part_z)

    sent_y, sent_z = stack((part_y, y0), (part_z, r1))
    a1, r2, far_a = ring(sent_y), ring(r1), across(sent_z)
    parts = [one(y0, 1, 0), [own_z] + one(r1, 0, 1)]
    acc = project("more", scalars, parts, held, weights, [2, 3, 4], acc)
    acc, a1, r2, far_a = in_order(acc, a1, r2, far_a)

    a2, r3, far2 = ring(a1), ring(r2), across(r2)
    parts = [two(a1, 1), one(r2, 0, 2) + [(x, at(1, i)) for i, (x, _) in enumerate(two(far_a, 0))]]
    acc = project("more", scalars, parts, held, weights, [5, 6], acc)
    acc, a2, r3, far2 = in_order(acc, a2, r3, far2)

    a3, far3 = ring(a2), across(r3)
    parts = [two(a2, 2), one(r3, 0, 3) + one(far2, 1, 2)]
    acc = project("more", scalars, parts, held, weights, [7], acc)
    acc, a3, far3 = in_order(acc, a3, far3)

    last_y, last_z = [two(a3, 3)], [one(far3, 1, 3)]
    keys_y, values_y, sent_y = project("kv", scalars, last_y, held, accs=acc[:2])
    one_y = swapped(sent_y, 1)
    acc, state_y = in_order(acc, sent_y)
    keys_z, values_z, sent_z = project(
        "kv", scalars, last_z, held, accs=acc[4:6], first_seq=half
    )
    above_z = ahead(sent_z, 4)
    acc, state_z = in_order(acc, sent_z)
    query_y, inner_y, gate_y = project(
        "qg", scalars, last_y, held, accs=acc[2:4], extra=(keys_y, values_y, gain)
    )
    query_y, one_y, acc = in_order(query_y, one_y, acc)
    pair_y = extend(pair_kernel, scalars, state_y, one_y, 0)
    two_y = swapped(pair_y, 2)
    above_z, pair_y = in_order(above_z, pair_y)
    chosen = choose(scalars, state_z, above_z)
    around_z = [round_x(x, distance) for distance, x in enumerate(chosen, 1)]
    acc, chosen = in_order(acc, chosen)
    query_z, inner_z, gate_z = project(
        "qg", scalars, last_z, held, accs=acc[6:], extra=(keys_z, values_z, gain), first_seq=half
    )
    query_z, two_y = in_order(query_z, two_y)
    four_y = ahead(extend(quad_kernel, scalars, pair_y, two_y, 0), 4)
    query_z, around_z = in_order(query_z, around_z)
    attn_z, squares_z = combine(False, scalars, query_z, inner_z, (*around_z, above_z), half)
    squares_z, four_y = in_order(squares_z, four_y)
    attn_y, squares_y = combine(True, scalars, query_y, inner_y, (one_y, two_y, four_y), 0)
    squares = all_sum(join(squares_y, squares_z))
    return finish((attn_y, attn_z), (gate_y, gate_z), squares)


def solution(mesh):
    in_specs = (
        P(None, "ctx", "tp"),
        P(None, "tp"),
        P(None, "tp"),
        P(None, "tp"),
        P(None, "tp"),
        P("tp"),
        P("tp"),
        P(),
    )
    out_specs = P(None, "ctx", "tp")
    return jax.shard_map(
        on_device, mesh=mesh, in_specs=in_specs, out_specs=out_specs, check_vma=False
    )
```
